512 devices in a mesh: row: 16 (over y, core), col: 32 (over x, z).
Axes of the slice: x: 4, y: 8, z: 8, core: 2. Of those that a mesh axis runs over, the one named last changes fastest.
Arguments:
- covariance: float32 [9216, 9216], P('row', 'col'), may hold values from -1 to 10, as said below
- samples: float32 [192, 9216], P(None, ('col', 'row')), may hold values from -2 to 2
- labels: int32 [192], replicated, may hold values from 0 to 1023
- weights: float32 [9216, 1024], P(('col', 'row')), may hold values from -2.5 to 2.5
Outputs:
- new_covariance: float32 [9216, 9216], P('row', 'col')
- new_weights: float32 [9216, 1024], P(('col', 'row'))
The draws below stay inside these ranges and needn't reach their ends.
Inputs may be any that keep to these rules, and one draw needn't show every extreme that they name: covariance is symmetric and positive definite.
All inputs are finite; a program needn't handle non-finite values.
Results may differ from the reference program's by a relative error of at most 0.00005.
Values sent between devices are 32-bit elements; how exact they have to be, the bound alone decides.
A program may use at most 64 MiB of HBM per device.

```python
import math
import jax
import jax.numpy as jnp
from jax import lax

D = 9216
CLASSES = 1024
SAMPLES = 192


def draw_covariance(key, part):
    normals = jax.random.normal(key, (D, D), jnp.float32)
    noise = (normals + normals.T) * (0.4 / math.sqrt(2.0 * D))
    matrix = noise + jnp.eye(D, dtype=jnp.float32)
    return matrix


def draw_samples(key, part):
    spread = math.sqrt(8.0 / D)
    normals = jnp.clip(jax.random.normal(jax.random.fold_in(key, 11), (SAMPLES, D), jnp.float32), -6.0, 6.0)
    row_scales = jnp.exp(jax.random.uniform(jax.random.fold_in(key, 13), (SAMPLES,), jnp.float32, -2.0, 1.0))
    return normals * spread * row_scales[:, None]


def with_ends(array, stream_key, least, high):
    longest = array.shape.index(max(array.shape))
    spots = []
    for shift in (0, 1):
        where = [jax.random.randint(jax.random.fold_in(stream_key, axis), (), 0, length) for axis, length in enumerate(array.shape)]
        where[longest] = (where[longest] + shift) % array.shape[longest]
        spots.append(tuple(where))
    return array.at[spots[0]].set(least).at[spots[1]].set(high)


def steps_of(rng, shape, split, smallest, high):
    level, own = 1.0, jax.random.fold_in(rng, 6)
    for position, blocks in split:
        steps = jnp.exp(jax.random.uniform(jax.random.fold_in(own, position), (blocks,), jnp.float32, smallest / len(split), high / len(split)))
        level = level * jnp.repeat(steps, shape[position] // blocks).reshape([-1 if axis == position else 1 for axis in range(len(shape))])
    return level


def gaussian(stream_key, dims, scale, bound, split=(), kind=jnp.bfloat16):
    array = scale * jax.random.normal(stream_key, dims, jnp.float32)
    if split:
        array = array * steps_of(stream_key, dims, split, -0.22, 0.18)
    return jnp.clip(array, -bound, bound).astype(kind)


def setup_inputs(seed: int = 0) -> dict:
    streams_of = jax.random.split(jax.random.key(seed), 5)
    return {
        "covariance": draw_covariance(jax.random.fold_in(streams_of[4], 71), 0),
        "samples": draw_samples(jax.random.fold_in(streams_of[4], 71), 0),
        "labels": with_ends(jax.random.randint(streams_of[2], (SAMPLES,), 0, CLASSES), jax.random.fold_in(streams_of[2], 1), 0, CLASSES - 1).astype(jnp.int32),
        "weights": gaussian(streams_of[3], (D, CLASSES), 0.35, 2.5, ((0, 512),), jnp.float32),
    }


def reference(covariance, samples, labels, weights):
    precise = lax.Precision.HIGHEST
    products = jnp.dot(samples.astype(jnp.float32), covariance.astype(jnp.float32), precision=precise, preferred_element_type=jnp.float32)
    inner = jnp.dot(samples.astype(jnp.float32), products.T.astype(jnp.float32), precision=precise, preferred_element_type=jnp.float32)
    innovation = 0.5 * (inner + inner.T) + jnp.eye(SAMPLES, dtype=jnp.float32)
    factor = jnp.linalg.cholesky(innovation)
    gain = jax.scipy.linalg.cho_solve((factor, True), products)
    new_covariance = covariance - jnp.dot(products.T.astype(jnp.float32), gain.astype(jnp.float32), precision=precise, preferred_element_type=jnp.float32)
    classes = lax.broadcasted_iota(jnp.int32, (SAMPLES, CLASSES), 1)
    targets = (labels[:, None] == classes).astype(jnp.float32)
    predicted = jnp.dot(samples.astype(jnp.float32), weights.astype(jnp.float32), precision=precise, preferred_element_type=jnp.float32)
    new_weights = weights + jnp.dot(gain.T.astype(jnp.float32), (targets - predicted).astype(jnp.float32), precision=precise, preferred_element_type=jnp.float32)
    return (new_covariance, new_weights)
```

```python
import functools

import jax
import jax.numpy as jnp
from jax import lax
from jax.experimental import pallas as pl
from jax.experimental.pallas import tpu as pltpu
from jax.sharding import Mesh
from jax.sharding import PartitionSpec as P

MESH = pl.DeviceIdType.MESH
HIGH = lax.Precision.HIGHEST
F32 = jnp.float32

NY, NK, NX, NZ = 8, 2, 4, 8
B = 192
F = 18
FP = 24
CF, RF = 288, 576
XF = 144
C = 1024
CY = C // NY
SR, DR = 32, 24
AR = SR + DR


def dot(a, b, dims=(((1,), (0,)), ((), ()))):
    return lax.dot_general(a, b, dims, precision=HIGH, preferred_element_type=F32)


TN = (((0,), (0,)), ((), ()))
NT = (((1,), (1,)), ((), ()))


def exchange_kernel(
    cov, xin, win,
    s_out, pr_out, pc_out, pd_out,
    rt, rtp, rp, xpad, wst, xg, x8, x8c, wg, ts, tr, tx, tp, tzr, pz, prc,
    ar, arr, a1, azr, ayr, asum,
    lsem, ssem, s_xy, s_xk, s_x8, s_w, s_t, s_ar, s_tz, s_az, s_ay, s_pz, s_pc, s_pck, s_px, s_s, s_d,
):
    y, k, x, z = (lax.axis_index(a) for a in ("y", "k", "x", "z"))
    col = NZ * x + z
    row = 2 * y + k

    def at(yy=None, kk=None, xx=None, zz=None):
        ids = {}
        for name, v in (("y", yy), ("k", kk), ("x", xx), ("z", zz)):
            if v is not None:
                ids[name] = v
        return ids

    def other(v, d, n):
        return lax.rem(v + d, n)

    sent = []

    def send(src, dst, sem, to, when=None):
        cp = pltpu.make_async_remote_copy(src, dst, ssem, sem, device_id=to, device_id_type=MESH)
        cp.start()
        sent.append(cp)

    fy, fk, fx, fi = col // 4, (col // 2) % 2, 2 * (col % 2) + row // 8, row % 8
    x_is_own = (fy == y) & (fk == k) & (fx == x)
    pcol = 2 * row + x // 2
    gx, gz, gk, gj = pcol // NZ, pcol % NZ, z % 2, 4 * (x % 2) + z // 2
    p_is_own = (gx == x) & (gz == z) & (gk == k)

    barrier = pltpu.get_barrier_semaphore()

    def tell(to):
        pl.semaphore_signal(barrier, inc=1, device_id=to, device_id_type=MESH)

    for d in range(1, NY):
        tell(at(yy=other(y, d, NY)))
    for d in range(1, NZ):
        tell(at(zz=other(z, d, NZ)))
    for d in range(1, 8):
        tell(at(xx=other(x, d // 2, NX), kk=other(k, d % 2, NK)))

    def far_source(i):
        c = 2 * row + x // 2
        return 4 * (x % 2) + i // 2, i % 2, c // NZ, c % NZ

    def far_p_source(j):
        q = 2 * j + k
        return col // 4, (col // 2) % 2, 2 * (col % 2) + q // 8, q % 8

    for i in range(8):
        sy, sk, sx, sz = far_source(i)

        @pl.when(jnp.logical_not((sy == y) & (sk == k) & (sx == x) & (sz == z)))
        def _():
            tell(at(sy, sk, sx, sz))

        py, pk, px, pz_ = far_p_source(i)

        @pl.when(jnp.logical_not((py == y) & (pk == k) & (px == x) & (pz_ == z)))
        def _():
            tell(at(py, pk, px, pz_))

    load = pltpu.make_async_copy(cov, rt, lsem)
    load.start()
    xpad[...] = jnp.zeros_like(xpad)
    xpad[0:F, :] = xin[...]
    xg[k, y] = xpad[...]
    wst[...] = jnp.zeros_like(wst)
    for j in range(NY):
        wst[j, 0:F, :] = win[:, CY * j : CY * (j + 1)]
    wg[y] = wst[y]
    load.wait()
    rtp[...] = jnp.zeros_like(rtp)
    for q in range(16):
        r = 2 * (q % 8) + q // 8
        rtp[FP * q : FP * q + F, :] = rt[F * r : F * r + F, :]
    rp[...] = rtp[...].T

    own = x_is_own.astype(jnp.int32) + p_is_own.astype(jnp.int32)
    pl.semaphore_wait(barrier, 7 + 7 + 7 + 16 - own)

    for d in range(1, NY):
        send(xpad, xg.at[k, y], s_xy.at[d], at(yy=other(y, d, NY)))
    far = []
    for d in range(NZ):
        tz = other(z, d, NZ)
        if d == 0:

            @pl.when(x_is_own)
            def _():
                pltpu.make_async_copy(xpad, x8.at[fi], s_x8.at[fi]).start()

            @pl.when(jnp.logical_not(x_is_own))
            def _():
                pltpu.make_async_remote_copy(
                    xpad, x8.at[fi], ssem, s_x8.at[fi], device_id=at(fy, fk, fx, tz), device_id_type=MESH
                ).start()
        else:
            send(xpad, x8.at[fi], s_x8.at[fi], at(fy, fk, fx, tz))
    for d in range(1, NY):
        ty = other(y, d, NY)
        send(wst.at[ty], wg.at[y], s_w.at[d], at(yy=ty))

    def got(dst, sem):
        pltpu.make_async_copy(dst, dst, sem).wait()

    for d in range(1, NY):
        got(xpad, s_xy.at[d])
    send(xg.at[k], xg.at[k], s_xk, at(kk=1 - k))
    for d in range(1, NY):
        got(wg.at[0], s_w.at[d])
    part = dot(xg[k].reshape(NY * FP, B), wg[...].reshape(NY * FP, CY), TN)
    for q in range(8):
        ar[q, SR:AR, :] = part[DR * q : DR * (q + 1), :]
    got(xg.at[0], s_xk)

    xct = xg[...].reshape(2 * NY * FP, B)
    for d in (2, 1, 3, 0):
        tx_ = other(x, d, NX)
        ts[d] = dot(rp[pl.ds(pl.multiple_of(XF * tx_, 16), XF), :], xct)
        if d:
            send(ts.at[d], tr.at[d], s_t.at[d], at(xx=tx_))
    for i in range(8):
        got(xpad, s_x8.at[i])
    for i in range(8):
        x8c[F * i : F * (i + 1), :] = x8[i, 0:F, :]
    for d in range(1, NX):
        got(tr.at[d], s_t.at[d])
    tx[...] = ts[0] + tr[1] + tr[2] + tr[3]
    inner = dot(x8c[...], tx[...], TN)
    for q in range(4):
        ar[q, 0:SR, :] = inner[SR * q : SR * (q + 1), 0:128]
    for q in range(2):
        ar[4 + q, 0:SR, :] = inner[128 + SR * q : 128 + SR * (q + 1), 0:128]
        ar[6 + q, 0:SR, :] = jnp.zeros((SR, 128), F32)
        ar[6 + q, 0:SR, 0:64] = inner[128 + SR * q : 128 + SR * (q + 1), 128:192]
    for d in range(1, 8):
        tx_, tk_ = other(x, d // 2, NX), other(k, d % 2, NK)
        send(ar.at[2 * tx_ + tk_], arr.at[d], s_ar.at[d], at(xx=tx_, kk=tk_))
    tp[...] = jnp.zeros_like(tp)
    for i in range(8):
        tp[i, 0:F, :] = tx[F * i : F * (i + 1), :]
    for d in range(1, NZ):
        tz = other(z, d, NZ)
        send(tp.at[tz], tzr.at[d], s_tz.at[d], at(zz=tz))

    for d in range(1, 8):
        got(arr.at[d], s_ar.at[d])
    q_own = 2 * x + k
    total = ar[q_own]
    for d in range(1, 8):
        total = total + arr[d]
    a1[...] = total
    for d in range(1, NZ):
        send(a1, azr.at[d], s_az.at[d], at(zz=other(z, d, NZ)))

    for d in range(1, NZ):
        got(tzr.at[d], s_tz.at[d])
    piece = tp[z]
    for d in range(1, NZ):
        piece = piece + tzr[d]
    pz[z] = piece
    for d in range(1, NZ):
        send(pz.at[z], pz.at[z], s_pz.at[d], at(zz=other(z, d, NZ)))
    for d in range(NY):
        ty = other(y, d, NY)
        if d == 0:

            @pl.when(p_is_own)
            def _():
                pltpu.make_async_copy(pz.at[z], pc_out.at[gk, gj], s_pc.at[gj]).start()

            @pl.when(jnp.logical_not(p_is_own))
            def _():
                pltpu.make_async_remote_copy(
                    pz.at[z], pc_out.at[gk, gj], ssem, s_pc.at[gj], device_id=at(ty, gk, gx, gz), device_id_type=MESH
                ).start()
        else:
            send(pz.at[z], pc_out.at[gk, gj], s_pc.at[gj], at(ty, gk, gx, gz))

    for d in range(1, NZ):
        got(azr.at[d], s_az.at[d])
    total = a1[...]
    for d in range(1, NZ):
        total = total + azr[d]
    ayr[y] = total
    for d in range(1, NY):
        send(ayr.at[y], ayr.at[y], s_ay.at[d], at(yy=other(y, d, NY)))

    for d in range(1, NZ):
        got(pz.at[0], s_pz.at[d])
    for i in range(8):
        prc[F * i : F * (i + 1), :] = pz[i, 0:F, :]
    pr_out[x] = prc[...]
    for d in range(1, NX):
        send(prc, pr_out.at[x], s_px.at[d], at(xx=other(x, d, NX)))

    for d in range(1, NY):
        got(ayr.at[0], s_ay.at[d])
    total = ayr[0, 0:SR, :]
    for j in range(1, NY):
        total = total + ayr[j, 0:SR, :]
    asum[...] = total
    s_out[q_own] = total
    pd_out[q_own] = ayr[:, SR:AR, :]
    for d in range(1, 8):
        send(asum, s_out.at[q_own], s_s.at[d], at(xx=other(x, d // 2, NX), kk=other(k, d % 2, NK)))
    for d in range(1, 8):
        send(
            ayr.at[:, pl.ds(SR, DR), :], pd_out.at[q_own], s_d.at[d], at(xx=other(x, d // 2, NX), kk=other(k, d % 2, NK))
        )

    for i in range(8):
        got(xpad, s_pc.at[i])
    send(pc_out.at[k], pc_out.at[k], s_pck, at(kk=1 - k))
    for d in range(1, 8):
        got(asum, s_s.at[d])
    for d in range(1, NX):
        got(prc, s_px.at[d])
    for d in range(1, 8):
        got(pd_out.at[0], s_d.at[d])
    got(pc_out.at[0], s_pck)
    for cp in sent:
        cp.wait_send()

    @pl.when(jnp.logical_not(x_is_own))
    def _():
        got(xpad, ssem)

    @pl.when(jnp.logical_not(p_is_own))
    def _():
        got(xpad, ssem)


def wide(v, n):
    return jnp.broadcast_to(v, (8, n))


def inverse_of_2(a, b, d):
    s = 1.0 / (a * d - b * b)
    return ((d * s, -(b * s)), (-(b * s), a * s))


def inverse_of_4(d):
    two = range(2)
    p = inverse_of_2(d[0][0], d[0][1], d[1][1])
    w = [[p[i][0] * d[0][2 + j] + p[i][1] * d[1][2 + j] for j in two] for i in two]
    s = [[d[2 + i][2 + j] - (d[0][2 + i] * w[0][j] + d[1][2 + i] * w[1][j]) for j in two] for i in two]
    q = inverse_of_2(s[0][0], s[0][1], s[1][1])
    v = [[w[i][0] * q[0][j] + w[i][1] * q[1][j] for j in two] for i in two]
    m = [[None] * 4 for _ in range(4)]
    for i in two:
        for j in two:
            m[2 + i][2 + j] = q[i][j]
            m[i][2 + j] = -v[i][j]
            m[2 + j][i] = -v[i][j]
            m[i][j] = p[i][j] + v[i][0] * w[j][0] + v[i][1] * w[j][1]
    return m


def inverse_of_block(block):
    n = block.shape[0]
    lane = lax.broadcasted_iota(jnp.int32, (8, n), 1)
    sub = lax.broadcasted_iota(jnp.int32, (8, n), 0)
    tiles = [block[8 * t : 8 * t + 8, :] for t in range(n // 8)]
    four = range(4)
    for j in range(0, n, 4):
        t0, s0 = j // 8, j % 8
        cols = [[wide(t[:, j + a : j + a + 1], n) for a in four] for t in tiles]
        rows = [wide(tiles[t0][s0 + a : s0 + a + 1, :], n) for a in four]
        m = inverse_of_4([[wide(cols[t0][c][s0 + a : s0 + a + 1, :], n) for c in four] for a in four])
        inside = (lane >= j) & (lane < j + 4)
        rows = [jnp.where(inside, jnp.where(lane == j + a, 1.0, 0.0), rows[a]) for a in four]
        g = [m[a][0] * rows[0] + m[a][1] * rows[1] + (m[a][2] * rows[2] + m[a][3] * rows[3]) for a in four]
        for t in range(n // 8):
            v = jnp.where(inside, 0.0, tiles[t])
            for a in four:
                v = v - cols[t][a] * g[a]
            if t == t0:
                for a in four:
                    v = jnp.where(sub == s0 + a, g[a], v)
            tiles[t] = v
    return jnp.concatenate(tiles, axis=0)


def update_kernel(s, pr, pc, pd, cov, w, labels, cov_out, w_out, a, pcc, dd):
    y = lax.axis_index("y")
    k = lax.axis_index("k")
    h = 64
    top = s[0:4].reshape(128, 128)
    low = s[4:6].reshape(h, 128)
    end = s[6:8].reshape(h, 128)[:, 0:h]
    eye = (
        lax.broadcasted_iota(jnp.int32, (B, B), 0) == lax.broadcasted_iota(jnp.int32, (B, B), 1)
    ).astype(F32)
    a[0:128, 0:128] = 0.5 * (top + top.T)
    a[128:192, 0:128] = low
    a[0:128, 128:192] = low.T
    a[128:192, 128:192] = 0.5 * (end + end.T)
    a[...] = a[...] + eye
    for n in range(3):
        lo = h * n
        panel = a[lo : lo + h, :]
        inv = inverse_of_block(panel[:, lo : lo + h])
        g = dot(inv, panel)
        for m in range(3):
            if m != n:
                c = a[h * m : h * m + h, lo : lo + h]
                a[h * m : h * m + h, :] = a[h * m : h * m + h, :] - dot(c, g)
                a[h * m : h * m + h, lo : lo + h] = -dot(c, inv)
        a[lo : lo + h, :] = g
        a[lo : lo + h, lo : lo + h] = inv
    for r in range(16):
        pcc[F * r : F * (r + 1), :] = pc[r % 2, r // 2, 0:F, :]
    named = jnp.broadcast_to(labels[...].astype(F32), (128, B)).T
    lane = lax.broadcasted_iota(jnp.int32, (B, 128), 1).astype(F32)
    for j in range(NY):
        for q in range(8):
            at = slice(DR * q, DR * (q + 1))
            dd[at, CY * j : CY * (j + 1)] = (named[at] == lane[at] + float(CY * j)).astype(F32) - pd[q, j]
    inv = a[...]
    gain = dot(pcc[...], inv)
    cov_out[...] = cov[...] - dot(gain, pr[...].reshape(RF, B), NT)
    own = dot(pc[k, y], inv)
    w_out[...] = w[...] + dot(own, dd[...])[0:F]


def vmem(shape):
    return pltpu.VMEM(shape, F32)


def on_device(covariance, samples, labels, weights):
    in_vmem = pl.BlockSpec(memory_space=pltpu.VMEM)
    cov_t = covariance.T
    sems = lambda n: pltpu.SemaphoreType.DMA((n,))
    one = pltpu.SemaphoreType.DMA
    s, pr, pc, pd = pl.pallas_call(
        exchange_kernel,
        name="exchange",
        out_shape=(
            jax.ShapeDtypeStruct((8, SR, 128), F32),
            jax.ShapeDtypeStruct((NX, XF, B), F32),
            jax.ShapeDtypeStruct((2, NY, FP, B), F32),
            jax.ShapeDtypeStruct((8, NY, DR, CY), F32),
        ),
        in_specs=[pl.BlockSpec(memory_space=pl.ANY), in_vmem, in_vmem],
        out_specs=(in_vmem,) * 4,
        scratch_shapes=[
            vmem((CF, RF)), vmem((16 * FP, RF)), vmem((RF, 16 * FP)),
            vmem((FP, B)), vmem((NY, FP, CY)), vmem((2, NY, FP, B)), vmem((8, FP, B)), vmem((XF, B)),
            vmem((NY, FP, CY)), vmem((NX, XF, B)), vmem((NX, XF, B)), vmem((XF, B)), vmem((NZ, FP, B)),
            vmem((NZ, FP, B)), vmem((NZ, FP, B)), vmem((XF, B)),
            vmem((8, AR, 128)), vmem((8, AR, 128)), vmem((AR, 128)), vmem((NZ, AR, 128)), vmem((NY, AR, 128)),
            vmem((SR, 128)),
            one, one, sems(8), one, sems(8), sems(8), sems(4), sems(8), sems(8), sems(8), sems(8), sems(8), sems(8),
            one, sems(4), sems(8), sems(8),
        ],
        compiler_params=pltpu.CompilerParams(
            collective_id=0, has_side_effects=True, vmem_limit_bytes=40 * 2**20
        ),
    )(cov_t, samples.T, weights)
    cov_new, w_new = pl.pallas_call(
        update_kernel,
        name="update",
        out_shape=(jax.ShapeDtypeStruct((CF, RF), F32), jax.ShapeDtypeStruct((F, C), F32)),
        in_specs=[in_vmem] * 7,
        out_specs=(in_vmem,) * 2,
        scratch_shapes=[vmem((B, B)), vmem((CF, B)), vmem((B, C))],
        compiler_params=pltpu.CompilerParams(vmem_limit_bytes=40 * 2**20),
    )(s, pr, pc, pd, cov_t, weights, labels.reshape(1, B))
    return cov_new.T, w_new


def solution(mesh):
    finer = Mesh(mesh.devices.reshape(NY, NK, NX, NZ), ("y", "k", "x", "z"))
    row, col, both = ("y", "k"), ("x", "z"), ("x", "z", "y", "k")
    in_specs = (P(row, col), P(None, both), P(), P(both, None))
    out_specs = (P(row, col), P(both, None))
    return jax.shard_map(on_device, mesh=finer, in_specs=in_specs, out_specs=out_specs, check_vma=False)
```

```python
import functools

import jax
import jax.numpy as jnp
from jax import lax
from jax.experimental import pallas as pl
from jax.experimental.pallas import tpu as pltpu
from jax.sharding import Mesh
from jax.sharding import PartitionSpec as P

MESH = pl.DeviceIdType.MESH
HIGH = lax.Precision.HIGHEST
F32 = jnp.float32

NY, NK, NX, NZ = 8, 2, 4, 8
B = 192
F = 18
FP = 24
CF, RF = 288, 576
XF = 144
C = 1024
CY = C // NY
SR, DR = 32, 24
AR = SR + DR


def dot(a, b, dims=(((1,), (0,)), ((), ()))):
    return lax.dot_general(a, b, dims, precision=HIGH, preferred_element_type=F32)


TN = (((0,), (0,)), ((), ()))
NT = (((1,), (1,)), ((), ()))


def wide(v, n):
    return jnp.broadcast_to(v, (8, n))


def inverse_of_2(a, b, d):
    s = 1.0 / (a * d - b * b)
    return ((d * s, -(b * s)), (-(b * s), a * s))


def inverse_of_4(d):
    two = range(2)
    p = inverse_of_2(d[0][0], d[0][1], d[1][1])
    w = [[p[i][0] * d[0][2 + j] + p[i][1] * d[1][2 + j] for j in two] for i in two]
    s = [[d[2 + i][2 + j] - (d[0][2 + i] * w[0][j] + d[1][2 + i] * w[1][j]) for j in two] for i in two]
    q = inverse_of_2(s[0][0], s[0][1], s[1][1])
    v = [[w[i][0] * q[0][j] + w[i][1] * q[1][j] for j in two] for i in two]
    m = [[None] * 4 for _ in range(4)]
    for i in two:
        for j in two:
            m[2 + i][2 + j] = q[i][j]
            m[i][2 + j] = -v[i][j]
            m[2 + j][i] = -v[i][j]
            m[i][j] = p[i][j] + v[i][0] * w[j][0] + v[i][1] * w[j][1]
    return m


def inverse_of_block(block):
    n = block.shape[0]
    lane = lax.broadcasted_iota(jnp.int32, (8, n), 1)
    sub = lax.broadcasted_iota(jnp.int32, (8, n), 0)
    tiles = [block[8 * t : 8 * t + 8, :] for t in range(n // 8)]
    four = range(4)
    for j in range(0, n, 4):
        t0, s0 = j // 8, j % 8
        cols = [[wide(t[:, j + a : j + a + 1], n) for a in four] for t in tiles]
        rows = [wide(tiles[t0][s0 + a : s0 + a + 1, :], n) for a in four]
        m = inverse_of_4([[wide(cols[t0][c][s0 + a : s0 + a + 1, :], n) for c in four] for a in four])
        inside = (lane >= j) & (lane < j + 4)
        rows = [jnp.where(inside, jnp.where(lane == j + a, 1.0, 0.0), rows[a]) for a in four]
        g = [m[a][0] * rows[0] + m[a][1] * rows[1] + (m[a][2] * rows[2] + m[a][3] * rows[3]) for a in four]
        for t in range(n // 8):
            v = jnp.where(inside, 0.0, tiles[t])
            for a in four:
                v = v - cols[t][a] * g[a]
            if t == t0:
                for a in four:
                    v = jnp.where(sub == s0 + a, g[a], v)
            tiles[t] = v
    return jnp.concatenate(tiles, axis=0)


def pivot_block(a, h, n):
    lo = h * n
    panel = a[lo : lo + h, :]
    inv = inverse_of_block(panel[:, lo : lo + h])
    g = dot(inv, panel)
    for m in range(a.shape[0] // h):
        if m != n:
            c = a[h * m : h * m + h, lo : lo + h]
            a[h * m : h * m + h, :] = a[h * m : h * m + h, :] - dot(c, g)
            a[h * m : h * m + h, lo : lo + h] = -dot(c, inv)
    a[lo : lo + h, :] = g
    a[lo : lo + h, lo : lo + h] = inv


def exchange_kernel(
    cov, xin, win,
    inv_out, pr_out, pc_out, pd_out,
    s_out, rt, rtp, rp, xpad, wst, xg, x8, x8c, wg, ts, tr, tx, tp, tzr, pz, prc,
    ar, arr, a1, azr, ayr, asum,
    lsem, ssem, s_xy, s_xk, s_xf, s_x8, s_w, s_t, s_ar, s_tz, s_az, s_ay, s_pz, s_pf, s_pc, s_pck, s_px, s_s, s_d, s_dk,
):
    y, k, x, z = (lax.axis_index(a) for a in ("y", "k", "x", "z"))
    col = NZ * x + z
    row = 2 * y + k

    def at(yy=None, kk=None, xx=None, zz=None):
        ids = {}
        for name, v in (("y", yy), ("k", kk), ("x", xx), ("z", zz)):
            if v is not None:
                ids[name] = v
        return ids

    def other(v, d, n):
        return lax.rem(v + d, n)

    sent, coming = [], {}

    def send(src, dst, sem, to, slot=None, expect=True):
        land = sem if slot is None else sem.at[slot]
        cp = pltpu.make_async_remote_copy(src, dst, ssem, land, device_id=to, device_id_type=MESH)
        cp.start()
        sent.append(cp)
        if expect:
            coming[id(sem), slot] = src, land

    def got(sem, *slots):
        for slot in slots or (None,):
            src, land = coming.pop((id(sem), slot))
            pltpu.make_async_copy(src, src, land).wait()

    fy, fk, fx, fi = col // 4, (col // 2) % 2, 2 * (col % 2) + row // 8, row % 8
    pcol = 2 * row + x // 2
    gy, gk, gx, gz = 4 * (x % 2) + z // 2, z % 2, pcol // NZ, pcol % NZ
    is_own = (fy == y) & (fk == k) & (fx == x) & (fi == z)

    barrier = pltpu.get_barrier_semaphore()

    def tell(to):
        pl.semaphore_signal(barrier, inc=1, device_id=to, device_id_type=MESH)

    for d in range(1, NY):
        tell(at(yy=other(y, d, NY)))
    for d in range(1, NZ):
        tell(at(zz=other(z, d, NZ)))
    for d in range(1, 8):
        tell(at(xx=other(x, d // 2, NX), kk=other(k, d % 2, NK)))

    @pl.when(jnp.logical_not(is_own))
    def _():
        tell(at(gy, gk, gx, gz))
        tell(at(fy, fk, fx, fi))

    load = pltpu.make_async_copy(cov, rt, lsem)
    load.start()
    xpad[...] = jnp.zeros_like(xpad)
    xpad[0:F, :] = xin[...]
    xg[k, y] = xpad[...]
    wst[...] = jnp.zeros_like(wst)
    for j in range(NY):
        wst[j, 0:F, :] = win[:, CY * j : CY * (j + 1)]
    wg[y] = wst[y]
    load.wait()
    rtp[...] = jnp.zeros_like(rtp)
    for q in range(16):
        r = 2 * (q % 8) + q // 8
        rtp[FP * q : FP * q + F, :] = rt[F * r : F * r + F, :]
    rp[...] = rtp[...].T

    pl.semaphore_wait(barrier, 7 + 7 + 7 + 2 - 2 * is_own.astype(jnp.int32))

    for d in range(1, NY):
        send(xpad, xg.at[k, y], s_xy, at(yy=other(y, d, NY)), d)

    def send_far(src, dst, sem, to):
        @pl.when(is_own)
        def _():
            pltpu.make_async_copy(src, dst, sem).start()

        @pl.when(jnp.logical_not(is_own))
        def _():
            pltpu.make_async_remote_copy(src, dst, ssem, sem, device_id=to, device_id_type=MESH).start()

        coming[id(sem), None] = src, sem

    send_far(xpad, x8.at[fi], s_xf, at(fy, fk, fx, fi))

    got(s_xy, *range(1, NY))
    send(xg.at[k], xg.at[k], s_xk, at(kk=1 - k))
    for d in range(1, NY):
        ty = other(y, d, NY)
        send(wst.at[ty], wg.at[y], s_w, at(yy=ty), d)
    got(s_xk)
    xct = xg[...].reshape(2 * NY * FP, B)
    for d in (2, 1, 3, 0):
        tx_ = other(x, d, NX)
        ts[d] = dot(rp[pl.ds(pl.multiple_of(XF * tx_, 16), XF), :], xct)
        if d:
            send(ts.at[d], tr.at[d], s_t, at(xx=tx_), d)
    got(s_xf)
    for d in range(1, NZ):
        send(x8.at[z], x8.at[z], s_x8, at(zz=other(z, d, NZ)), d)
    got(s_w, *range(1, NY))
    part = dot(xg[k].reshape(NY * FP, B), wg[...].reshape(NY * FP, CY), TN)
    for q in range(8):
        ar[q, SR:AR, :] = part[DR * q : DR * (q + 1), :]
    got(s_x8, *range(1, 8))
    for i in range(8):
        x8c[F * i : F * (i + 1), :] = x8[i, 0:F, :]
    got(s_t, *range(1, NX))
    tx[...] = ts[0] + tr[1] + tr[2] + tr[3]
    inner = dot(x8c[...], tx[...], TN)
    for q in range(4):
        ar[q, 0:SR, :] = inner[SR * q : SR * (q + 1), 0:128]
    for q in range(2):
        ar[4 + q, 0:SR, :] = inner[128 + SR * q : 128 + SR * (q + 1), 0:128]
        ar[6 + q, 0:SR, :] = jnp.zeros((SR, 128), F32)
        ar[6 + q, 0:SR, 0:64] = inner[128 + SR * q : 128 + SR * (q + 1), 128:192]
    for d in range(1, 8):
        tx_, tk_ = other(x, d // 2, NX), other(k, d % 2, NK)
        send(ar.at[2 * tx_ + tk_], arr.at[d], s_ar, at(xx=tx_, kk=tk_), d)
    tp[...] = jnp.zeros_like(tp)
    for i in range(8):
        tp[i, 0:F, :] = tx[F * i : F * (i + 1), :]
    for d in range(1, NZ):
        tz = other(z, d, NZ)
        send(tp.at[tz], tzr.at[d], s_tz, at(zz=tz), d)

    got(s_ar, *range(1, 8))
    q_own = 2 * x + k
    total = ar[q_own]
    for d in range(1, 8):
        total = total + arr[d]
    a1[...] = total
    for d in range(1, NZ):
        send(a1, azr.at[d], s_az, at(zz=other(z, d, NZ)), d)

    got(s_az, *range(1, NZ))
    total = a1[...]
    for d in range(1, NZ):
        total = total + azr[d]
    ayr[y] = total
    for d in range(1, NY):
        send(ayr.at[y], ayr.at[y], s_ay, at(yy=other(y, d, NY)), d)

    got(s_tz, *range(1, NZ))
    piece = tp[z]
    for d in range(1, NZ):
        piece = piece + tzr[d]
    pz[z] = piece
    for d in range(1, NZ):
        send(pz.at[z], pz.at[z], s_pz, at(zz=other(z, d, NZ)), d)
    send_far(pz.at[z], pc_out.at[gk, gy], s_pf, at(gy, gk, gx, gz))

    got(s_ay, *range(1, NY))
    total = ayr[0, 0:SR, :]
    for j in range(1, NY):
        total = total + ayr[j, 0:SR, :]
    asum[...] = total
    s_out[q_own] = total
    for d in range(1, 8):
        send(asum, s_out.at[q_own], s_s, at(xx=other(x, d // 2, NX), kk=other(k, d % 2, NK)), d)
    got(s_pz, *range(1, NZ))
    for i in range(8):
        prc[F * i : F * (i + 1), :] = pz[i, 0:F, :]
    pr_out[x] = prc[...]
    for d in range(1, NX):
        send(prc, pr_out.at[x], s_px, at(xx=other(x, d, NX)), d)
    got(s_pf)
    for d in range(1, NY):
        send(pc_out.at[k, y], pc_out.at[k, y], s_pc, at(yy=other(y, d, NY)), d)
    pd_out[k, x] = ayr[:, SR:AR, :]
    for d in range(1, NX):
        send(pd_out.at[k, x], pd_out.at[k, x], s_d, at(xx=other(x, d, NX)), d)

    got(s_s, *range(1, 8))
    h = 64
    top = s_out[0:4].reshape(128, 128)
    low = s_out[4:6].reshape(h, 128)
    end = s_out[6:8].reshape(h, 128)[:, 0:h]
    eye = (
        lax.broadcasted_iota(jnp.int32, (B, B), 0) == lax.broadcasted_iota(jnp.int32, (B, B), 1)
    ).astype(F32)
    inv_out[0:128, 0:128] = 0.5 * (top + top.T)
    inv_out[128:192, 0:128] = low
    inv_out[0:128, 128:192] = low.T
    inv_out[128:192, 128:192] = 0.5 * (end + end.T)
    inv_out[...] = inv_out[...] + eye
    for n in range(3):
        pivot_block(inv_out, h, n)
        if n == 0:
            got(s_pc, *range(1, 8))
            send(pc_out.at[k], pc_out.at[k], s_pck, at(kk=1 - k))
            got(s_d, *range(1, NX))
            send(pd_out.at[k], pd_out.at[k], s_dk, at(kk=1 - k))
    got(s_px, *range(1, NX))
    got(s_pck)
    got(s_dk)
    for cp in sent:
        cp.wait_send()

    @pl.when(jnp.logical_not(is_own))
    def _():
        pltpu.make_async_copy(xpad, xpad, ssem).wait()
        pltpu.make_async_copy(xpad, xpad, ssem).wait()


def update_kernel(inv, pr, pc, pd, cov, w, labels, cov_out, w_out, pcc, dd):
    y = lax.axis_index("y")
    k = lax.axis_index("k")
    for r in range(16):
        pcc[F * r : F * (r + 1), :] = pc[r % 2, r // 2, 0:F, :]
    named = jnp.broadcast_to(labels[...].astype(F32), (128, B)).T
    lane = lax.broadcasted_iota(jnp.int32, (B, 128), 1).astype(F32)
    for j in range(NY):
        for q in range(8):
            at = slice(DR * q, DR * (q + 1))
            dd[at, CY * j : CY * (j + 1)] = (named[at] == lane[at] + float(CY * j)).astype(F32) - pd[q % 2, q // 2, j]
    gain = dot(pcc[...], inv[...])
    cov_out[...] = cov[...] - dot(gain, pr[...].reshape(RF, B), NT)
    own = dot(pc[k, y], inv[...])
    w_out[...] = w[...] + dot(own, dd[...])[0:F]


def vmem(shape):
    return pltpu.VMEM(shape, F32)


def on_device(covariance, samples, labels, weights):
    in_vmem = pl.BlockSpec(memory_space=pltpu.VMEM)
    cov_t = covariance.T
    sems = lambda n: pltpu.SemaphoreType.DMA((n,))
    one = pltpu.SemaphoreType.DMA
    inv, pr, pc, pd = pl.pallas_call(
        exchange_kernel,
        name="exchange",
        out_shape=(
            jax.ShapeDtypeStruct((B, B), F32),
            jax.ShapeDtypeStruct((NX, XF, B), F32),
            jax.ShapeDtypeStruct((2, NY, FP, B), F32),
            jax.ShapeDtypeStruct((2, NX, NY, DR, CY), F32),
        ),
        in_specs=[pl.BlockSpec(memory_space=pl.ANY), in_vmem, in_vmem],
        out_specs=(in_vmem,) * 4,
        scratch_shapes=[
            vmem((8, SR, 128)), vmem((CF, RF)), vmem((16 * FP, RF)), vmem((RF, 16 * FP)),
            vmem((FP, B)), vmem((NY, FP, CY)), vmem((2, NY, FP, B)), vmem((8, FP, B)), vmem((XF, B)),
            vmem((NY, FP, CY)), vmem((NX, XF, B)), vmem((NX, XF, B)), vmem((XF, B)), vmem((NZ, FP, B)),
            vmem((NZ, FP, B)), vmem((NZ, FP, B)), vmem((XF, B)),
            vmem((8, AR, 128)), vmem((8, AR, 128)), vmem((AR, 128)), vmem((NZ, AR, 128)), vmem((NY, AR, 128)),
            vmem((SR, 128)),
            one, one, sems(8), one, one, sems(8), sems(8), sems(4), sems(8), sems(8), sems(8), sems(8), sems(8), one, sems(8),
            one, sems(4), sems(8), sems(4), one,
        ],
        compiler_params=pltpu.CompilerParams(
            collective_id=0, has_side_effects=True, vmem_limit_bytes=40 * 2**20
        ),
    )(cov_t, samples.T, weights)
    cov_new, w_new = pl.pallas_call(
        update_kernel,
        name="update",
        out_shape=(jax.ShapeDtypeStruct((CF, RF), F32), jax.ShapeDtypeStruct((F, C), F32)),
        in_specs=[in_vmem] * 7,
        out_specs=(in_vmem,) * 2,
        scratch_shapes=[vmem((CF, B)), vmem((B, C))],
        compiler_params=pltpu.CompilerParams(vmem_limit_bytes=40 * 2**20),
    )(inv, pr, pc, pd, cov_t, weights, labels.reshape(1, B))
    return cov_new.T, w_new


def solution(mesh):
    finer = Mesh(mesh.devices.reshape(NY, NK, NX, NZ), ("y", "k", "x", "z"))
    row, col, both = ("y", "k"), ("x", "z"), ("x", "z", "y", "k")
    in_specs = (P(row, col), P(None, both), P(), P(both, None))
    out_specs = (P(row, col), P(both, None))
    return jax.shard_map(on_device, mesh=finer, in_specs=in_specs, out_specs=out_specs, check_vma=False)
```

```python
import functools

import jax
import jax.numpy as jnp
from jax import lax
from jax.experimental import pallas as pl
from jax.experimental.pallas import tpu as pltpu
from jax.sharding import Mesh
from jax.sharding import PartitionSpec as P

MESH = pl.DeviceIdType.MESH
HIGH = lax.Precision.HIGHEST
F32 = jnp.float32

NY, NK, NX, NZ = 8, 2, 4, 8
B = 192
F = 18
FP = 24
PP = 32
CF, RF = 288, 576
XF = 144
C = 1024
CY = C // NY
XR = XF + XF // 2
SR, DR = 32, 24


def dot(a, b, dims=(((1,), (0,)), ((), ()))):
    return lax.dot_general(a, b, dims, precision=HIGH, preferred_element_type=F32)


TN = (((0,), (0,)), ((), ()))
NT = (((1,), (1,)), ((), ()))


def wide(v, n):
    return jnp.broadcast_to(v, (8, n))


def inverse_of_2(a, b, d):
    s = 1.0 / (a * d - b * b)
    return ((d * s, -(b * s)), (-(b * s), a * s))


def inverse_of_4(d):
    two = range(2)
    p = inverse_of_2(d[0][0], d[0][1], d[1][1])
    w = [[p[i][0] * d[0][2 + j] + p[i][1] * d[1][2 + j] for j in two] for i in two]
    s = [[d[2 + i][2 + j] - (d[0][2 + i] * w[0][j] + d[1][2 + i] * w[1][j]) for j in two] for i in two]
    q = inverse_of_2(s[0][0], s[0][1], s[1][1])
    v = [[w[i][0] * q[0][j] + w[i][1] * q[1][j] for j in two] for i in two]
    m = [[None] * 4 for _ in range(4)]
    for i in two:
        for j in two:
            m[2 + i][2 + j] = q[i][j]
            m[i][2 + j] = -v[i][j]
            m[2 + j][i] = -v[i][j]
            m[i][j] = p[i][j] + v[i][0] * w[j][0] + v[i][1] * w[j][1]
    return m


def inverse_of_block(block):
    n = block.shape[0]
    lane = lax.broadcasted_iota(jnp.int32, (8, n), 1)
    sub = lax.broadcasted_iota(jnp.int32, (8, n), 0)
    tiles = [block[8 * t : 8 * t + 8, :] for t in range(n // 8)]
    four = range(4)
    for j in range(0, n, 4):
        t0, s0 = j // 8, j % 8
        cols = [[wide(t[:, j + a : j + a + 1], n) for a in four] for t in tiles]
        rows = [wide(tiles[t0][s0 + a : s0 + a + 1, :], n) for a in four]
        m = inverse_of_4([[wide(cols[t0][c][s0 + a : s0 + a + 1, :], n) for c in four] for a in four])
        inside = (lane >= j) & (lane < j + 4)
        rows = [jnp.where(inside, jnp.where(lane == j + a, 1.0, 0.0), rows[a]) for a in four]
        g = [m[a][0] * rows[0] + m[a][1] * rows[1] + (m[a][2] * rows[2] + m[a][3] * rows[3]) for a in four]
        for t in range(n // 8):
            v = jnp.where(inside, 0.0, tiles[t])
            for a in four:
                v = v - cols[t][a] * g[a]
            if t == t0:
                for a in four:
                    v = jnp.where(sub == s0 + a, g[a], v)
            tiles[t] = v
    return jnp.concatenate(tiles, axis=0)


def fold(ref, at, rows, row):
    ref[(*at, slice(0, F), slice(None))] = rows[row : row + F, 0:128]
    ref[(*at, slice(F, F + 9), slice(0, 64))] = rows[row : row + 9, 128:192]
    ref[(*at, slice(F, F + 9), slice(64, 128))] = rows[row + 9 : row + F, 128:192]


def unfold(ref, at, row, piece):
    ref[(*at, slice(row, row + F), slice(0, 128))] = piece[0:F]
    ref[(*at, slice(row, row + 9), slice(128, 192))] = piece[F : F + 9, 0:64]
    ref[(*at, slice(row + 9, row + F), slice(128, 192))] = piece[F : F + 9, 64:128]


def pivot_block(a, h, n):
    lo = h * n
    panel = a[lo : lo + h, :]
    inv = inverse_of_block(panel[:, lo : lo + h])
    g = dot(inv, panel)
    for m in range(a.shape[0] // h):
        if m != n:
            c = a[h * m : h * m + h, lo : lo + h]
            a[h * m : h * m + h, :] = a[h * m : h * m + h, :] - dot(c, g)
            a[h * m : h * m + h, lo : lo + h] = -dot(c, inv)
    a[lo : lo + h, :] = g
    a[lo : lo + h, lo : lo + h] = inv


def exchange_kernel(
    cov, xin, win,
    inv_out, pr_out, pc_out, pd_out, rt, wt,
    s_out, xt, rtp, rp, xpad, wst, xg, xu, x8, x8c, wg, ts, tr, tx, tp, tzr, pz, prc,
    ar, arr, a1, azr, ayr, asum, dr, drr, d1, dzr, dyr,
    lsem, ssem, s_xy, s_xk, s_xf, s_x8, s_w, s_t, s_ar, s_tz, s_az, s_ay, s_pz, s_pf, s_pc, s_pck, s_px, s_s, s_d, s_dk,
    s_dx, s_dz, s_dy,
):
    y, k, x, z = (lax.axis_index(a) for a in ("y", "k", "x", "z"))
    col = NZ * x + z
    row = 2 * y + k

    def at(yy=None, kk=None, xx=None, zz=None):
        ids = {}
        for name, v in (("y", yy), ("k", kk), ("x", xx), ("z", zz)):
            if v is not None:
                ids[name] = v
        return ids

    def other(v, d, n):
        return lax.rem(v + d, n)

    sent, coming = [], {}

    def send(src, dst, sem, to, slot=None, expect=True):
        land = sem if slot is None else sem.at[slot]
        cp = pltpu.make_async_remote_copy(src, dst, ssem, land, device_id=to, device_id_type=MESH)
        cp.start()
        sent.append(cp)
        if expect:
            coming[id(sem), slot] = src, land

    def got(sem, *slots):
        for slot in slots or (None,):
            src, land = coming.pop((id(sem), slot))
            pltpu.make_async_copy(src, src, land).wait()

    fy, fk, fx, fi = col // 4, (col // 2) % 2, 2 * (col % 2) + row // 8, row % 8
    pcol = 2 * row + x // 2
    gy, gk, gx, gz = 4 * (x % 2) + z // 2, z % 2, pcol // NZ, pcol % NZ
    is_own = (fy == y) & (fk == k) & (fx == x) & (fi == z)

    barrier = pltpu.get_barrier_semaphore()

    def tell(to):
        pl.semaphore_signal(barrier, inc=1, device_id=to, device_id_type=MESH)

    for d in range(1, NY):
        tell(at(yy=other(y, d, NY)))
    for d in range(1, NZ):
        tell(at(zz=other(z, d, NZ)))
    for d in range(1, 8):
        tell(at(xx=other(x, d // 2, NX), kk=other(k, d % 2, NK)))

    @pl.when(jnp.logical_not(is_own))
    def _():
        tell(at(gy, gk, gx, gz))
        tell(at(fy, fk, fx, fi))

    loads = [pltpu.make_async_copy(f, t, lsem.at[i]) for i, (f, t) in enumerate(((xin, xt), (win, wt), (cov, rt)))]
    for load in loads:
        load.start()
    xpad[...] = jnp.zeros_like(xpad)
    xu[...] = jnp.zeros_like(xu)
    tp[...] = jnp.zeros_like(tp)
    wst[...] = jnp.zeros_like(wst)
    loads[0].wait()
    fold(xpad, (), xt, 0)
    xg[k, y] = xpad[...]
    loads[1].wait()
    for j in range(NY):
        wst[j, 0:F, :] = wt[:, CY * j : CY * (j + 1)]
    wg[y] = wst[y]
    loads[2].wait()
    rtp[...] = jnp.zeros_like(rtp)
    for q in range(16):
        r = 2 * (q % 8) + q // 8
        rtp[FP * q : FP * q + F, :] = rt[F * r : F * r + F, :]
    rp[...] = rtp[...].T

    pl.semaphore_wait(barrier, 7 + 7 + 7 + 2 - 2 * is_own.astype(jnp.int32))

    for d in range(1, NY):
        send(xpad, xg.at[k, y], s_xy, at(yy=other(y, d, NY)), d)

    def send_far(src, dst, sem, to):
        @pl.when(is_own)
        def _():
            pltpu.make_async_copy(src, dst, sem).start()

        @pl.when(jnp.logical_not(is_own))
        def _():
            pltpu.make_async_remote_copy(src, dst, ssem, sem, device_id=to, device_id_type=MESH).start()

        coming[id(sem), None] = src, sem

    send_far(xpad, x8.at[fi], s_xf, at(fy, fk, fx, fi))

    got(s_xy, *range(1, NY))
    send(xg.at[k], xg.at[k], s_xk, at(kk=1 - k))
    for d in range(1, NY):
        ty = other(y, d, NY)
        send(wst.at[ty], wg.at[y], s_w, at(yy=ty), d)
    for j in range(NY):
        unfold(xu, (k,), FP * j, xg[k, j])
    got(s_xk)
    for j in range(NY):
        unfold(xu, (1 - k,), FP * j, xg[1 - k, j])
    xct = xu[...].reshape(2 * NY * FP, B)
    for d in (2, 1, 3, 0):
        tx_ = other(x, d, NX)
        t = dot(rp[pl.ds(pl.multiple_of(XF * tx_, 16), XF), :], xct)
        ts[d, 0:XF, :] = t[:, 0:128]
        for i in range(8):
            ts[d, XF + 9 * i : XF + 9 * i + 9, 0:64] = t[F * i : F * i + 9, 128:192]
            ts[d, XF + 9 * i : XF + 9 * i + 9, 64:128] = t[F * i + 9 : F * i + F, 128:192]
        if d:
            send(ts.at[d], tr.at[d], s_t, at(xx=tx_), d)
    got(s_xf)
    for d in range(1, NZ):
        send(x8.at[z], x8.at[z], s_x8, at(zz=other(z, d, NZ)), d)
    got(s_w, *range(1, NY))
    part = dot(xu[k], wg[...].reshape(NY * FP, CY), TN)
    for q in range(8):
        dr[q] = part[DR * q : DR * (q + 1), :]
    got(s_x8, *range(1, 8))
    for i in range(8):
        unfold(x8c, (), F * i, x8[i])
    got(s_t, *range(1, NX))
    ts[0] = ts[0] + tr[1] + tr[2] + tr[3]
    tx[:, 0:128] = ts[0, 0:XF, :]
    for i in range(8):
        tx[F * i : F * i + 9, 128:192] = ts[0, XF + 9 * i : XF + 9 * i + 9, 0:64]
        tx[F * i + 9 : F * i + F, 128:192] = ts[0, XF + 9 * i : XF + 9 * i + 9, 64:128]
    inner = dot(x8c[...], tx[...], TN)
    for q in range(4):
        ar[q] = inner[SR * q : SR * (q + 1), 0:128]
    for q in range(2):
        ar[4 + q] = inner[128 + SR * q : 128 + SR * (q + 1), 0:128]
        ar[6 + q] = jnp.zeros((SR, 128), F32)
        ar[6 + q, :, 0:64] = inner[128 + SR * q : 128 + SR * (q + 1), 128:192]
    for d in range(1, 8):
        tx_, tk_ = other(x, d // 2, NX), other(k, d % 2, NK)
        send(ar.at[2 * tx_ + tk_], arr.at[d], s_ar, at(xx=tx_, kk=tk_), d)
    for d in range(1, 8):
        tx_, tk_ = other(x, d // 2, NX), other(k, d % 2, NK)
        send(dr.at[2 * tx_ + tk_], drr.at[d], s_dx, at(xx=tx_, kk=tk_), d)
    for i in range(8):
        tp[i, 0:F, :] = ts[0, F * i : F * (i + 1), :]
        tp[i, F : F + 9, :] = ts[0, XF + 9 * i : XF + 9 * i + 9, :]
    for d in range(1, NZ):
        tz = other(z, d, NZ)
        send(tp.at[tz], tzr.at[d], s_tz, at(zz=tz), d)

    got(s_ar, *range(1, 8))
    q_own = 2 * x + k
    total = ar[q_own]
    for d in range(1, 8):
        total = total + arr[d]
    a1[...] = total
    for d in range(1, NZ):
        send(a1, azr.at[d], s_az, at(zz=other(z, d, NZ)), d)
    got(s_dx, *range(1, 8))
    total = dr[q_own]
    for d in range(1, 8):
        total = total + drr[d]
    d1[...] = total
    for d in range(1, NZ):
        send(d1, dzr.at[d], s_dz, at(zz=other(z, d, NZ)), d)

    got(s_az, *range(1, NZ))
    total = a1[...]
    for d in range(1, NZ):
        total = total + azr[d]
    ayr[y] = total
    for d in range(1, NY):
        send(ayr.at[y], ayr.at[y], s_ay, at(yy=other(y, d, NY)), d)

    got(s_dz, *range(1, NZ))
    total = d1[...]
    for d in range(1, NZ):
        total = total + dzr[d]
    dyr[y] = total
    for d in range(1, NY):
        send(dyr.at[y], dyr.at[y], s_dy, at(yy=other(y, d, NY)), d)
    got(s_tz, *range(1, NZ))
    piece = tp[z]
    for d in range(1, NZ):
        piece = piece + tzr[d]
    pz[z] = piece
    for d in range(1, NZ):
        send(pz.at[z], pz.at[z], s_pz, at(zz=other(z, d, NZ)), d)
    send_far(pz.at[z], pc_out.at[gk, gy], s_pf, at(gy, gk, gx, gz))

    got(s_ay, *range(1, NY))
    total = ayr[0]
    for j in range(1, NY):
        total = total + ayr[j]
    asum[...] = total
    s_out[q_own] = total
    for d in range(1, 8):
        send(asum, s_out.at[q_own], s_s, at(xx=other(x, d // 2, NX), kk=other(k, d % 2, NK)), d)
    got(s_pz, *range(1, NZ))
    for i in range(8):
        prc[F * i : F * (i + 1), :] = pz[i, 0:F, :]
        prc[XF + 9 * i : XF + 9 * i + 9, :] = pz[i, F : F + 9, :]
    pr_out[x] = prc[...]
    for d in range(1, NX):
        send(prc, pr_out.at[x], s_px, at(xx=other(x, d, NX)), d)
    got(s_pf)
    for d in range(1, NY):
        send(pc_out.at[k, y], pc_out.at[k, y], s_pc, at(yy=other(y, d, NY)), d)
    got(s_dy, *range(1, NY))
    pd_out[k, x] = dyr[...]
    for d in range(1, NX):
        send(pd_out.at[k, x], pd_out.at[k, x], s_d, at(xx=other(x, d, NX)), d)

    got(s_s, *range(1, 8))
    h = 64
    top = s_out[0:4].reshape(128, 128)
    low = s_out[4:6].reshape(h, 128)
    end = s_out[6:8].reshape(h, 128)[:, 0:h]
    eye = (
        lax.broadcasted_iota(jnp.int32, (B, B), 0) == lax.broadcasted_iota(jnp.int32, (B, B), 1)
    ).astype(F32)
    inv_out[0:128, 0:128] = 0.5 * (top + top.T)
    inv_out[128:192, 0:128] = low
    inv_out[0:128, 128:192] = low.T
    inv_out[128:192, 128:192] = 0.5 * (end + end.T)
    inv_out[...] = inv_out[...] + eye
    for n in range(3):
        pivot_block(inv_out, h, n)
        if n == 0:
            got(s_pc, *range(1, 8))
            send(pc_out.at[k], pc_out.at[k], s_pck, at(kk=1 - k))
            got(s_d, *range(1, NX))
            send(pd_out.at[k], pd_out.at[k], s_dk, at(kk=1 - k))
    got(s_px, *range(1, NX))
    got(s_pck)
    got(s_dk)
    for cp in sent:
        cp.wait_send()

    @pl.when(jnp.logical_not(is_own))
    def _():
        pltpu.make_async_copy(xpad, xpad, ssem).wait()
        pltpu.make_async_copy(xpad, xpad, ssem).wait()


def update_kernel(inv, pr, pc, pd, cov, w, labels, cov_out, w_out, pcc, dd, prc, pco):
    y = lax.axis_index("y")
    k = lax.axis_index("k")
    for r in range(16):
        unfold(pcc, (), F * r, pc[r % 2, r // 2])
    for j in range(NX):
        prc[j, :, 0:128] = pr[j, 0:XF, :]
        for i in range(8):
            prc[j, F * i : F * i + 9, 128:192] = pr[j, XF + 9 * i : XF + 9 * i + 9, 0:64]
            prc[j, F * i + 9 : F * i + F, 128:192] = pr[j, XF + 9 * i : XF + 9 * i + 9, 64:128]
    pco[...] = jnp.zeros_like(pco)
    unfold(pco, (), 0, pc[k, y])
    named = jnp.broadcast_to(labels[...].astype(F32), (128, B)).T
    lane = lax.broadcasted_iota(jnp.int32, (B, 128), 1).astype(F32)
    for j in range(NY):
        for q in range(8):
            at = slice(DR * q, DR * (q + 1))
            dd[at, CY * j : CY * (j + 1)] = (named[at] == lane[at] + float(CY * j)).astype(F32) - pd[q % 2, q // 2, j]
    gain = dot(pcc[...], inv[...])
    cov_out[...] = cov[...] - dot(gain, prc[...].reshape(RF, B), NT)
    own = dot(pco[...], inv[...])
    w_out[...] = w[...] + dot(own, dd[...])[0:F]


def vmem(shape):
    return pltpu.VMEM(shape, F32)


def on_device(covariance, samples, labels, weights):
    in_vmem = pl.BlockSpec(memory_space=pltpu.VMEM)
    cov_t = covariance.T
    sems = lambda n: pltpu.SemaphoreType.DMA((n,))
    one = pltpu.SemaphoreType.DMA
    inv, pr, pc, pd, cov_in, w_in = pl.pallas_call(
        exchange_kernel,
        name="exchange",
        out_shape=tuple(
            jax.ShapeDtypeStruct(shape, F32)
            for shape in ((B, B), (NX, XR, 128), (2, NY, PP, 128), (2, NX, NY, DR, CY), (CF, RF), (F, C))
        ),
        in_specs=[pl.BlockSpec(memory_space=pltpu.HBM)] * 3,
        out_specs=(in_vmem,) * 6,
        scratch_shapes=[
            vmem((8, SR, 128)), vmem((F, B)), vmem((16 * FP, RF)), vmem((RF, 16 * FP)),
            vmem((PP, 128)), vmem((NY, FP, CY)), vmem((2, NY, PP, 128)), vmem((2, NY * FP, B)),
            vmem((8, PP, 128)), vmem((XF, B)), vmem((NY, FP, CY)),
            vmem((NX, XR, 128)), vmem((NX, XR, 128)), vmem((XF, B)), vmem((NZ, PP, 128)),
            vmem((NZ, PP, 128)), vmem((NZ, PP, 128)), vmem((XR, 128)),
            vmem((8, SR, 128)), vmem((8, SR, 128)), vmem((SR, 128)), vmem((NZ, SR, 128)), vmem((NY, SR, 128)),
            vmem((SR, 128)),
            vmem((8, DR, 128)), vmem((8, DR, 128)), vmem((DR, 128)), vmem((NZ, DR, 128)), vmem((NY, DR, 128)),
            sems(3), one, sems(8), one, one, sems(8), sems(8), sems(4), sems(8), sems(8), sems(8), sems(8), sems(8),
            one, sems(8), one, sems(4), sems(8), sems(4), one, sems(8), sems(8), sems(8),
        ],
        compiler_params=pltpu.CompilerParams(
            collective_id=0, has_side_effects=True, vmem_limit_bytes=40 * 2**20
        ),
    )(cov_t, samples.T, weights)
    cov_new, w_new = pl.pallas_call(
        update_kernel,
        name="update",
        out_shape=(jax.ShapeDtypeStruct((CF, RF), F32), jax.ShapeDtypeStruct((F, C), F32)),
        in_specs=[in_vmem] * 7,
        out_specs=(in_vmem,) * 2,
        scratch_shapes=[vmem((CF, B)), vmem((B, C)), vmem((NX, XF, B)), vmem((FP, B))],
        compiler_params=pltpu.CompilerParams(vmem_limit_bytes=40 * 2**20),
    )(inv, pr, pc, pd, cov_in, w_in, labels.reshape(1, B))
    return cov_new.T, w_new


def solution(mesh):
    finer = Mesh(mesh.devices.reshape(NY, NK, NX, NZ), ("y", "k", "x", "z"))
    row, col, both = ("y", "k"), ("x", "z"), ("x", "z", "y", "k")
    in_specs = (P(row, col), P(None, both), P(), P(both, None))
    out_specs = (P(row, col), P(both, None))
    return jax.shard_map(on_device, mesh=finer, in_specs=in_specs, out_specs=out_specs, check_vma=False)
```

```python
import functools

import jax
import jax.numpy as jnp
from jax import lax
from jax.experimental import pallas as pl
from jax.experimental.pallas import tpu as pltpu
from jax.sharding import Mesh
from jax.sharding import PartitionSpec as P

MESH = pl.DeviceIdType.MESH
HIGH = lax.Precision.HIGHEST
F32 = jnp.float32

NY, NK, NX, NZ = 8, 2, 4, 8
B = 192
F = 18
FP = 24
PP = 32
CF, RF = 288, 576
XF = 144
C = 1024
CY = C // NY
XR = XF + XF // 2
SR, DR = 32, 24


def dot(a, b, dims=(((1,), (0,)), ((), ()))):
    return lax.dot_general(a, b, dims, precision=HIGH, preferred_element_type=F32)


TN = (((0,), (0,)), ((), ()))
NT = (((1,), (1,)), ((), ()))


def wide(v, n):
    return jnp.broadcast_to(v, (8, n))


def inverse_of_2(a, b, d):
    s = 1.0 / (a * d - b * b)
    return ((d * s, -(b * s)), (-(b * s), a * s))


def inverse_of_4(d):
    two = range(2)
    p = inverse_of_2(d[0][0], d[0][1], d[1][1])
    w = [[p[i][0] * d[0][2 + j] + p[i][1] * d[1][2 + j] for j in two] for i in two]
    s = [[d[2 + i][2 + j] - (d[0][2 + i] * w[0][j] + d[1][2 + i] * w[1][j]) for j in two] for i in two]
    q = inverse_of_2(s[0][0], s[0][1], s[1][1])
    v = [[w[i][0] * q[0][j] + w[i][1] * q[1][j] for j in two] for i in two]
    m = [[None] * 4 for _ in range(4)]
    for i in two:
        for j in two:
            m[2 + i][2 + j] = q[i][j]
            m[i][2 + j] = -v[i][j]
            m[2 + j][i] = -v[i][j]
            m[i][j] = p[i][j] + v[i][0] * w[j][0] + v[i][1] * w[j][1]
    return m


def product(a, b):
    out = []
    for row in a:
        line = []
        for j in range(len(b[0])):
            t = [row[i] * b[i][j] for i in range(len(b))]
            while len(t) > 1:
                t = [t[i] + t[i + 1] for i in range(0, len(t), 2)]
            line.append(t[0])
        out.append(line)
    return out


def flipped(a):
    return [list(r) for r in zip(*a)]


def inverse_of_8(d):
    four = range(4)
    p = inverse_of_4([r[:4] for r in d[:4]])
    q = [r[4:] for r in d[:4]]
    w = product(p, q)
    qw = product(flipped(q), w)
    i4 = inverse_of_4([[d[4 + i][4 + j] - qw[i][j] for j in four] for i in four])
    v = product(w, i4)
    u = product(v, flipped(w))
    m = [[None] * 8 for _ in range(8)]
    for i in four:
        for j in four:
            m[4 + i][4 + j] = i4[i][j]
            m[i][4 + j] = -v[i][j]
            m[4 + j][i] = -v[i][j]
            m[i][j] = p[i][j] + u[i][j]
    return m


def inverse_of_block(block):
    n = block.shape[0]
    lane = lax.broadcasted_iota(jnp.int32, (8, n), 1)
    sub = lax.broadcasted_iota(jnp.int32, (8, n), 0)
    tiles = [block[8 * t : 8 * t + 8, :] for t in range(n // 8)]
    eight = range(8)
    for t0 in range(n // 8):
        j = 8 * t0
        cols = [[wide(t[:, j + a : j + a + 1], n) for a in eight] for t in tiles]
        rows = [wide(tiles[t0][a : a + 1, :], n) for a in eight]
        pivots = [[None] * 8 for _ in eight]
        for a in eight:
            for c in range(a, 8):
                pivots[a][c] = pivots[c][a] = wide(cols[t0][c][a : a + 1, :], n)
        m = inverse_of_8(pivots)
        inside = (lane >= j) & (lane < j + 8)
        rows = [jnp.where(inside, jnp.where(lane == j + a, 1.0, 0.0), rows[a]) for a in eight]
        g = [r[0] for r in product(m, [[r] for r in rows])]
        for t in range(n // 8):
            if t == t0:
                v = g[0]
                for a in range(1, 8):
                    v = jnp.where(sub == a, g[a], v)
            else:
                v = jnp.where(inside, 0.0, tiles[t]) - product([cols[t]], [[r] for r in g])[0][0]
            tiles[t] = v
    return jnp.concatenate(tiles, axis=0)


def fold(ref, at, rows, row):
    ref[(*at, slice(0, F), slice(None))] = rows[row : row + F, 0:128]
    ref[(*at, slice(F, F + 9), slice(0, 64))] = rows[row : row + 9, 128:192]
    ref[(*at, slice(F, F + 9), slice(64, 128))] = rows[row + 9 : row + F, 128:192]


def unfold(ref, at, row, piece):
    ref[(*at, slice(row, row + F), slice(0, 128))] = piece[0:F]
    ref[(*at, slice(row, row + 9), slice(128, 192))] = piece[F : F + 9, 0:64]
    ref[(*at, slice(row + 9, row + F), slice(128, 192))] = piece[F : F + 9, 64:128]


def pivot_block(a, h, n):
    lo = h * n
    panel = a[lo : lo + h, :]
    inv = inverse_of_block(panel[:, lo : lo + h])
    g = dot(inv, panel)
    for m in range(a.shape[0] // h):
        if m != n:
            c = a[h * m : h * m + h, lo : lo + h]
            a[h * m : h * m + h, :] = a[h * m : h * m + h, :] - dot(c, g)
            a[h * m : h * m + h, lo : lo + h] = -dot(c, inv)
    a[lo : lo + h, :] = g
    a[lo : lo + h, lo : lo + h] = inv


def exchange_kernel(
    cov, xin, win,
    inv_out, pr_out, pc_out, pd_out, rt, wt,
    s_out, xt, rtp, rp, xpad, wst, xg, xu, x8, x8c, wg, ts, tr, tx, tp, tzr, pz, prc,
    ar, arr, a1, azr, ayr, asum, dr, drr, d1, dzr, dyr,
    lsem, ssem, s_xy, s_xk, s_xf, s_x8, s_w, s_t, s_ar, s_tz, s_az, s_ay, s_pz, s_pf, s_pc, s_pck, s_px, s_s, s_d, s_dk,
    s_dx, s_dz, s_dy,
):
    y, k, x, z = (lax.axis_index(a) for a in ("y", "k", "x", "z"))
    col = NZ * x + z
    row = 2 * y + k

    def at(yy=None, kk=None, xx=None, zz=None):
        ids = {}
        for name, v in (("y", yy), ("k", kk), ("x", xx), ("z", zz)):
            if v is not None:
                ids[name] = v
        return ids

    def other(v, d, n):
        return lax.rem(v + d, n)

    sent, coming = [], {}

    def send(src, dst, sem, to, slot=None, expect=True):
        land = sem if slot is None else sem.at[slot]
        cp = pltpu.make_async_remote_copy(src, dst, ssem, land, device_id=to, device_id_type=MESH)
        cp.start()
        sent.append(cp)
        if expect:
            coming[id(sem), slot] = src, land

    def got(sem, *slots):
        for slot in slots or (None,):
            src, land = coming.pop((id(sem), slot))
            pltpu.make_async_copy(src, src, land).wait()

    fy, fk, fx, fi = col // 4, (col // 2) % 2, 2 * (col % 2) + row // 8, row % 8
    pcol = 2 * row + x // 2
    gy, gk, gx, gz = 4 * (x % 2) + z // 2, z % 2, pcol // NZ, pcol % NZ
    is_own = (fy == y) & (fk == k) & (fx == x) & (fi == z)

    barrier = pltpu.get_barrier_semaphore()

    def tell(to):
        pl.semaphore_signal(barrier, inc=1, device_id=to, device_id_type=MESH)

    for d in range(1, NY):
        tell(at(yy=other(y, d, NY)))
    for d in range(1, NZ):
        tell(at(zz=other(z, d, NZ)))
    for d in range(1, 8):
        tell(at(xx=other(x, d // 2, NX), kk=other(k, d % 2, NK)))

    @pl.when(jnp.logical_not(is_own))
    def _():
        tell(at(gy, gk, gx, gz))
        tell(at(fy, fk, fx, fi))

    loads = [pltpu.make_async_copy(f, t, lsem.at[i]) for i, (f, t) in enumerate(((xin, xt), (win, wt), (cov, rt)))]
    for load in loads:
        load.start()
    xpad[...] = jnp.zeros_like(xpad)
    xu[...] = jnp.zeros_like(xu)
    tp[...] = jnp.zeros_like(tp)
    wst[...] = jnp.zeros_like(wst)
    loads[0].wait()
    fold(xpad, (), xt, 0)
    xg[k, y] = xpad[...]
    loads[1].wait()
    for j in range(NY):
        wst[j, 0:F, :] = wt[:, CY * j : CY * (j + 1)]
    wg[y] = wst[y]
    loads[2].wait()
    rtp[...] = jnp.zeros_like(rtp)
    for q in range(16):
        r = 2 * (q % 8) + q // 8
        rtp[FP * q : FP * q + F, :] = rt[F * r : F * r + F, :]
    rp[...] = rtp[...].T

    pl.semaphore_wait(barrier, 7 + 7 + 7 + 2 - 2 * is_own.astype(jnp.int32))

    for d in range(1, NY):
        send(xpad, xg.at[k, y], s_xy, at(yy=other(y, d, NY)), d)

    def send_far(src, dst, sem, to):
        @pl.when(is_own)
        def _():
            pltpu.make_async_copy(src, dst, sem).start()

        @pl.when(jnp.logical_not(is_own))
        def _():
            pltpu.make_async_remote_copy(src, dst, ssem, sem, device_id=to, device_id_type=MESH).start()

        coming[id(sem), None] = src, sem

    send_far(xpad, x8.at[fi], s_xf, at(fy, fk, fx, fi))

    got(s_xy, *range(1, NY))
    send(xg.at[k], xg.at[k], s_xk, at(kk=1 - k))
    for d in range(1, NY):
        ty = other(y, d, NY)
        send(wst.at[ty], wg.at[y], s_w, at(yy=ty), d)
    for j in range(NY):
        unfold(xu, (k,), FP * j, xg[k, j])
    got(s_xk)
    for j in range(NY):
        unfold(xu, (1 - k,), FP * j, xg[1 - k, j])
    xct = xu[...].reshape(2 * NY * FP, B)
    for d in (2, 1, 3, 0):
        tx_ = other(x, d, NX)
        t = dot(rp[pl.ds(pl.multiple_of(XF * tx_, 16), XF), :], xct)
        ts[d, 0:XF, :] = t[:, 0:128]
        for i in range(8):
            ts[d, XF + 9 * i : XF + 9 * i + 9, 0:64] = t[F * i : F * i + 9, 128:192]
            ts[d, XF + 9 * i : XF + 9 * i + 9, 64:128] = t[F * i + 9 : F * i + F, 128:192]
        if d:
            send(ts.at[d], tr.at[d], s_t, at(xx=tx_), d)
    got(s_xf)
    for d in range(1, NZ):
        send(x8.at[z], x8.at[z], s_x8, at(zz=other(z, d, NZ)), d)
    got(s_w, *range(1, NY))
    part = dot(xu[k], wg[...].reshape(NY * FP, CY), TN)
    for q in range(8):
        dr[q] = part[DR * q : DR * (q + 1), :]
    for d in range(1, 8):
        tx_, tk_ = other(x, d // 2, NX), other(k, d % 2, NK)
        send(dr.at[2 * tx_ + tk_], drr.at[d], s_dx, at(xx=tx_, kk=tk_), d)
    got(s_x8, *range(1, 8))
    for i in range(8):
        unfold(x8c, (), F * i, x8[i])
    got(s_t, *range(1, NX))
    ts[0] = ts[0] + tr[1] + tr[2] + tr[3]
    tx[:, 0:128] = ts[0, 0:XF, :]
    for i in range(8):
        tx[F * i : F * i + 9, 128:192] = ts[0, XF + 9 * i : XF + 9 * i + 9, 0:64]
        tx[F * i + 9 : F * i + F, 128:192] = ts[0, XF + 9 * i : XF + 9 * i + 9, 64:128]
    inner = dot(x8c[...], tx[...], TN)
    for q in range(4):
        ar[q] = inner[SR * q : SR * (q + 1), 0:128]
    for q in range(2):
        ar[4 + q] = inner[128 + SR * q : 128 + SR * (q + 1), 0:128]
        ar[6 + q] = jnp.zeros((SR, 128), F32)
        ar[6 + q, :, 0:64] = inner[128 + SR * q : 128 + SR * (q + 1), 128:192]
    for d in range(1, 8):
        tx_, tk_ = other(x, d // 2, NX), other(k, d % 2, NK)
        send(ar.at[2 * tx_ + tk_], arr.at[d], s_ar, at(xx=tx_, kk=tk_), d)
    q_own = 2 * x + k
    got(s_dx, *range(1, 8))
    total = dr[q_own]
    for d in range(1, 8):
        total = total + drr[d]
    d1[...] = total
    for d in range(1, NZ):
        send(d1, dzr.at[d], s_dz, at(zz=other(z, d, NZ)), d)

    got(s_ar, *range(1, 8))
    total = ar[q_own]
    for d in range(1, 8):
        total = total + arr[d]
    a1[...] = total
    for d in range(1, NZ):
        send(a1, azr.at[d], s_az, at(zz=other(z, d, NZ)), d)
    for i in range(8):
        tp[i, 0:F, :] = ts[0, F * i : F * (i + 1), :]
        tp[i, F : F + 9, :] = ts[0, XF + 9 * i : XF + 9 * i + 9, :]
    for d in range(1, NZ):
        tz = other(z, d, NZ)
        send(tp.at[tz], tzr.at[d], s_tz, at(zz=tz), d)
    got(s_dz, *range(1, NZ))
    total = d1[...]
    for d in range(1, NZ):
        total = total + dzr[d]
    dyr[y] = total
    for d in range(1, NY):
        send(dyr.at[y], dyr.at[y], s_dy, at(yy=other(y, d, NY)), d)

    got(s_az, *range(1, NZ))
    total = a1[...]
    for d in range(1, NZ):
        total = total + azr[d]
    ayr[y] = total
    for d in range(1, NY):
        send(ayr.at[y], ayr.at[y], s_ay, at(yy=other(y, d, NY)), d)
    got(s_tz, *range(1, NZ))
    piece = tp[z]
    for d in range(1, NZ):
        piece = piece + tzr[d]
    pz[z] = piece
    for d in range(1, NZ):
        send(pz.at[z], pz.at[z], s_pz, at(zz=other(z, d, NZ)), d)
    send_far(pz.at[z], pc_out.at[gk, gy], s_pf, at(gy, gk, gx, gz))
    got(s_dy, *range(1, NY))
    pd_out[k, x] = dyr[...]
    for d in range(1, NX):
        send(pd_out.at[k, x], pd_out.at[k, x], s_d, at(xx=other(x, d, NX)), d)


    got(s_ay, *range(1, NY))
    total = ayr[0]
    for j in range(1, NY):
        total = total + ayr[j]
    asum[...] = total
    s_out[q_own] = total
    for d in range(1, 8):
        send(asum, s_out.at[q_own], s_s, at(xx=other(x, d // 2, NX), kk=other(k, d % 2, NK)), d)
    got(s_pz, *range(1, NZ))
    for i in range(8):
        prc[F * i : F * (i + 1), :] = pz[i, 0:F, :]
        prc[XF + 9 * i : XF + 9 * i + 9, :] = pz[i, F : F + 9, :]
    pr_out[x] = prc[...]
    for d in range(1, NX):
        send(prc, pr_out.at[x], s_px, at(xx=other(x, d, NX)), d)
    got(s_pf)
    for d in range(1, NY):
        send(pc_out.at[k, y], pc_out.at[k, y], s_pc, at(yy=other(y, d, NY)), d)
    got(s_d, *range(1, NX))
    send(pd_out.at[k], pd_out.at[k], s_dk, at(kk=1 - k))

    got(s_s, *range(1, 8))
    h = 64
    top = s_out[0:4].reshape(128, 128)
    low = s_out[4:6].reshape(h, 128)
    end = s_out[6:8].reshape(h, 128)[:, 0:h]
    eye = (
        lax.broadcasted_iota(jnp.int32, (B, B), 0) == lax.broadcasted_iota(jnp.int32, (B, B), 1)
    ).astype(F32)
    inv_out[0:128, 0:128] = 0.5 * (top + top.T)
    inv_out[128:192, 0:128] = low
    inv_out[0:128, 128:192] = low.T
    inv_out[128:192, 128:192] = 0.5 * (end + end.T)
    inv_out[...] = inv_out[...] + eye
    for n in range(3):
        pivot_block(inv_out, h, n)
        if n == 0:
            got(s_pc, *range(1, 8))
            send(pc_out.at[k], pc_out.at[k], s_pck, at(kk=1 - k))
    got(s_px, *range(1, NX))
    got(s_pck)
    got(s_dk)
    for cp in sent:
        cp.wait_send()

    @pl.when(jnp.logical_not(is_own))
    def _():
        pltpu.make_async_copy(xpad, xpad, ssem).wait()
        pltpu.make_async_copy(xpad, xpad, ssem).wait()


def update_kernel(inv, pr, pc, pd, cov, w, labels, cov_out, w_out, pcc, dd, prc, pco):
    y = lax.axis_index("y")
    k = lax.axis_index("k")
    for r in range(16):
        unfold(pcc, (), F * r, pc[r % 2, r // 2])
    for j in range(NX):
        prc[j, :, 0:128] = pr[j, 0:XF, :]
        for i in range(8):
            prc[j, F * i : F * i + 9, 128:192] = pr[j, XF + 9 * i : XF + 9 * i + 9, 0:64]
            prc[j, F * i + 9 : F * i + F, 128:192] = pr[j, XF + 9 * i : XF + 9 * i + 9, 64:128]
    pco[...] = jnp.zeros_like(pco)
    unfold(pco, (), 0, pc[k, y])
    named = jnp.broadcast_to(labels[...].astype(F32), (128, B)).T
    lane = lax.broadcasted_iota(jnp.int32, (B, 128), 1).astype(F32)
    for j in range(NY):
        for q in range(8):
            at = slice(DR * q, DR * (q + 1))
            dd[at, CY * j : CY * (j + 1)] = (named[at] == lane[at] + float(CY * j)).astype(F32) - pd[q % 2, q // 2, j]
    gain = dot(pcc[...], inv[...])
    cov_out[...] = cov[...] - dot(gain, prc[...].reshape(RF, B), NT)
    own = dot(pco[...], inv[...])
    w_out[...] = w[...] + dot(own, dd[...])[0:F]


def vmem(shape):
    return pltpu.VMEM(shape, F32)


def on_device(covariance, samples, labels, weights):
    in_vmem = pl.BlockSpec(memory_space=pltpu.VMEM)
    cov_t = covariance.T
    sems = lambda n: pltpu.SemaphoreType.DMA((n,))
    one = pltpu.SemaphoreType.DMA
    inv, pr, pc, pd, cov_in, w_in = pl.pallas_call(
        exchange_kernel,
        name="exchange",
        out_shape=tuple(
            jax.ShapeDtypeStruct(shape, F32)
            for shape in ((B, B), (NX, XR, 128), (2, NY, PP, 128), (2, NX, NY, DR, CY), (CF, RF), (F, C))
        ),
        in_specs=[pl.BlockSpec(memory_space=pltpu.HBM)] * 3,
        out_specs=(in_vmem,) * 6,
        scratch_shapes=[
            vmem((8, SR, 128)), vmem((F, B)), vmem((16 * FP, RF)), vmem((RF, 16 * FP)),
            vmem((PP, 128)), vmem((NY, FP, CY)), vmem((2, NY, PP, 128)), vmem((2, NY * FP, B)),
            vmem((8, PP, 128)), vmem((XF, B)), vmem((NY, FP, CY)),
            vmem((NX, XR, 128)), vmem((NX, XR, 128)), vmem((XF, B)), vmem((NZ, PP, 128)),
            vmem((NZ, PP, 128)), vmem((NZ, PP, 128)), vmem((XR, 128)),
            vmem((8, SR, 128)), vmem((8, SR, 128)), vmem((SR, 128)), vmem((NZ, SR, 128)), vmem((NY, SR, 128)),
            vmem((SR, 128)),
            vmem((8, DR, 128)), vmem((8, DR, 128)), vmem((DR, 128)), vmem((NZ, DR, 128)), vmem((NY, DR, 128)),
            sems(3), one, sems(8), one, one, sems(8), sems(8), sems(4), sems(8), sems(8), sems(8), sems(8), sems(8),
            one, sems(8), one, sems(4), sems(8), sems(4), one, sems(8), sems(8), sems(8),
        ],
        compiler_params=pltpu.CompilerParams(
            collective_id=0, has_side_effects=True, vmem_limit_bytes=40 * 2**20
        ),
    )(cov_t, samples.T, weights)
    cov_new, w_new = pl.pallas_call(
        update_kernel,
        name="update",
        out_shape=(jax.ShapeDtypeStruct((CF, RF), F32), jax.ShapeDtypeStruct((F, C), F32)),
        in_specs=[in_vmem] * 7,
        out_specs=(in_vmem,) * 2,
        scratch_shapes=[vmem((CF, B)), vmem((B, C)), vmem((NX, XF, B)), vmem((FP, B))],
        compiler_params=pltpu.CompilerParams(vmem_limit_bytes=40 * 2**20),
    )(inv, pr, pc, pd, cov_in, w_in, labels.reshape(1, B))
    return cov_new.T, w_new


def solution(mesh):
    finer = Mesh(mesh.devices.reshape(NY, NK, NX, NZ), ("y", "k", "x", "z"))
    row, col, both = ("y", "k"), ("x", "z"), ("x", "z", "y", "k")
    in_specs = (P(row, col), P(None, both), P(), P(both, None))
    out_specs = (P(row, col), P(both, None))
    return jax.shard_map(on_device, mesh=finer, in_specs=in_specs, out_specs=out_specs, check_vma=False)
```

```python
import functools

import jax
import jax.numpy as jnp
from jax import lax
from jax.experimental import pallas as pl
from jax.experimental.pallas import tpu as pltpu
from jax.sharding import Mesh
from jax.sharding import PartitionSpec as P

MESH = pl.DeviceIdType.MESH
HIGH = lax.Precision.HIGHEST
F32 = jnp.float32

NY, NK, NX, NZ = 8, 2, 4, 8
B = 192
F = 18
FP = 24
PP = 32
CF, RF = 288, 576
XF = 144
C = 1024
CY = C // NY
XR = XF + XF // 2
SR, DR = 32, 24


def dot(a, b, dims=(((1,), (0,)), ((), ()))):
    return lax.dot_general(a, b, dims, precision=HIGH, preferred_element_type=F32)


TN = (((0,), (0,)), ((), ()))
NT = (((1,), (1,)), ((), ()))


def wide(v, n):
    return jnp.broadcast_to(v, (8, n))


def inverse_of_2(a, b, d):
    s = 1.0 / (a * d - b * b)
    return ((d * s, -(b * s)), (-(b * s), a * s))


def inverse_of_4(d):
    two = range(2)
    p = inverse_of_2(d[0][0], d[0][1], d[1][1])
    w = [[p[i][0] * d[0][2 + j] + p[i][1] * d[1][2 + j] for j in two] for i in two]
    s = [[d[2 + i][2 + j] - (d[0][2 + i] * w[0][j] + d[1][2 + i] * w[1][j]) for j in two] for i in two]
    q = inverse_of_2(s[0][0], s[0][1], s[1][1])
    v = [[w[i][0] * q[0][j] + w[i][1] * q[1][j] for j in two] for i in two]
    m = [[None] * 4 for _ in range(4)]
    for i in two:
        for j in two:
            m[2 + i][2 + j] = q[i][j]
            m[i][2 + j] = -v[i][j]
            m[2 + j][i] = -v[i][j]
            m[i][j] = p[i][j] + v[i][0] * w[j][0] + v[i][1] * w[j][1]
    return m


def product(a, b):
    out = []
    for row in a:
        line = []
        for j in range(len(b[0])):
            t = [row[i] * b[i][j] for i in range(len(b))]
            while len(t) > 1:
                t = [t[i] + t[i + 1] for i in range(0, len(t), 2)]
            line.append(t[0])
        out.append(line)
    return out


def flipped(a):
    return [list(r) for r in zip(*a)]


def inverse_of_8(d):
    four = range(4)
    p = inverse_of_4([r[:4] for r in d[:4]])
    q = [r[4:] for r in d[:4]]
    w = product(p, q)
    qw = product(flipped(q), w)
    i4 = inverse_of_4([[d[4 + i][4 + j] - qw[i][j] for j in four] for i in four])
    v = product(w, i4)
    u = product(v, flipped(w))
    m = [[None] * 8 for _ in range(8)]
    for i in four:
        for j in four:
            m[4 + i][4 + j] = i4[i][j]
            m[i][4 + j] = -v[i][j]
            m[4 + j][i] = -v[i][j]
            m[i][j] = p[i][j] + u[i][j]
    return m


def inverse_of_block(block):
    n = block.shape[0]
    lane = lax.broadcasted_iota(jnp.int32, (8, n), 1)
    sub = lax.broadcasted_iota(jnp.int32, (8, n), 0)
    tiles = [block[8 * t : 8 * t + 8, :] for t in range(n // 8)]
    eight = range(8)
    for t0 in range(n // 8):
        j = 8 * t0
        cols = [[wide(t[:, j + a : j + a + 1], n) for a in eight] for t in tiles]
        rows = [wide(tiles[t0][a : a + 1, :], n) for a in eight]
        pivots = [[None] * 8 for _ in eight]
        for a in eight:
            for c in range(a, 8):
                pivots[a][c] = pivots[c][a] = wide(cols[t0][c][a : a + 1, :], n)
        m = inverse_of_8(pivots)
        inside = (lane >= j) & (lane < j + 8)
        rows = [jnp.where(inside, jnp.where(lane == j + a, 1.0, 0.0), rows[a]) for a in eight]
        g = [r[0] for r in product(m, [[r] for r in rows])]
        for t in range(n // 8):
            if t == t0:
                v = g[0]
                for a in range(1, 8):
                    v = jnp.where(sub == a, g[a], v)
            else:
                v = jnp.where(inside, 0.0, tiles[t]) - product([cols[t]], [[r] for r in g])[0][0]
            tiles[t] = v
    return jnp.concatenate(tiles, axis=0)


def fold(ref, at, rows, row):
    ref[(*at, slice(0, F), slice(None))] = rows[row : row + F, 0:128]
    ref[(*at, slice(F, F + 9), slice(0, 64))] = rows[row : row + 9, 128:192]
    ref[(*at, slice(F, F + 9), slice(64, 128))] = rows[row + 9 : row + F, 128:192]


def unfold(ref, at, row, piece):
    ref[(*at, slice(row, row + F), slice(0, 128))] = piece[0:F]
    ref[(*at, slice(row, row + 9), slice(128, 192))] = piece[F : F + 9, 0:64]
    ref[(*at, slice(row + 9, row + F), slice(128, 192))] = piece[F : F + 9, 64:128]


def pivot_block(a, h, n):
    lo = h * n
    panel = a[lo : lo + h, :]
    inv = inverse_of_block(panel[:, lo : lo + h])
    g = dot(inv, panel)
    for m in range(a.shape[0] // h):
        if m != n:
            c = a[h * m : h * m + h, lo : lo + h]
            a[h * m : h * m + h, :] = a[h * m : h * m + h, :] - dot(c, g)
            a[h * m : h * m + h, lo : lo + h] = -dot(c, inv)
    a[lo : lo + h, :] = g
    a[lo : lo + h, lo : lo + h] = inv


def exchange_kernel(
    cov, xin, win,
    inv_out, pr_out, pc_out, pd_out, rt, wt,
    s_out, xt, rtp, rp, xpad, wst, xg, xu, x8, x8c, wg, th, ts, tr, tx, tp, tzr, pz, prc,
    ar, arr, a1, azr, ayr, asum, dr, drr, d1, dzr, dyr,
    lsem, ssem, s_xy, s_xk, s_xf, s_x8, s_w, s_t, s_ar, s_tz, s_az, s_ay, s_pz, s_pf, s_pc, s_pck, s_px, s_s, s_d, s_dk,
    s_dx, s_dz, s_dy,
):
    y, k, x, z = (lax.axis_index(a) for a in ("y", "k", "x", "z"))
    col = NZ * x + z
    row = 2 * y + k

    def at(yy=None, kk=None, xx=None, zz=None):
        ids = {}
        for name, v in (("y", yy), ("k", kk), ("x", xx), ("z", zz)):
            if v is not None:
                ids[name] = v
        return ids

    def other(v, d, n):
        return lax.rem(v + d, n)

    sent, coming = [], {}

    def send(src, dst, sem, to, slot=None, expect=True):
        land = sem if slot is None else sem.at[slot]
        cp = pltpu.make_async_remote_copy(src, dst, ssem, land, device_id=to, device_id_type=MESH)
        cp.start()
        sent.append(cp)
        if expect:
            coming[id(sem), slot] = src, land

    def got(sem, *slots):
        for slot in slots or (None,):
            src, land = coming.pop((id(sem), slot))
            pltpu.make_async_copy(src, src, land).wait()

    fy, fk, fx, fi = col // 4, (col // 2) % 2, 2 * (col % 2) + row // 8, row % 8
    pcol = 2 * row + x // 2
    gy, gk, gx, gz = 4 * (x % 2) + z // 2, z % 2, pcol // NZ, pcol % NZ
    is_own = (fy == y) & (fk == k) & (fx == x) & (fi == z)

    barrier = pltpu.get_barrier_semaphore()

    def tell(to):
        pl.semaphore_signal(barrier, inc=1, device_id=to, device_id_type=MESH)

    for d in range(1, NY):
        tell(at(yy=other(y, d, NY)))
    for d in range(1, NZ):
        tell(at(zz=other(z, d, NZ)))
    for d in range(1, 8):
        tell(at(xx=other(x, d // 2, NX), kk=other(k, d % 2, NK)))

    @pl.when(jnp.logical_not(is_own))
    def _():
        tell(at(gy, gk, gx, gz))
        tell(at(fy, fk, fx, fi))

    loads = [pltpu.make_async_copy(f, t, lsem.at[i]) for i, (f, t) in enumerate(((xin, xt), (win, wt), (cov, rt)))]
    for load in loads:
        load.start()
    xpad[...] = jnp.zeros_like(xpad)
    xu[...] = jnp.zeros_like(xu)
    tp[...] = jnp.zeros_like(tp)
    wst[...] = jnp.zeros_like(wst)
    loads[0].wait()
    fold(xpad, (), xt, 0)
    xg[k, y] = xpad[...]
    loads[1].wait()
    for j in range(NY):
        wst[j, 0:F, :] = wt[:, CY * j : CY * (j + 1)]
    wg[y] = wst[y]
    loads[2].wait()
    rtp[...] = jnp.zeros_like(rtp)
    for q in range(16):
        r = 2 * (q % 8) + q // 8
        rtp[FP * q : FP * q + F, :] = rt[F * r : F * r + F, :]
    for i in range(2):
        rp[i] = rtp[NY * FP * i : NY * FP * (i + 1), :].T

    pl.semaphore_wait(barrier, 7 + 7 + 7 + 2 - 2 * is_own.astype(jnp.int32))

    for d in range(1, NY):
        send(xpad, xg.at[k, y], s_xy, at(yy=other(y, d, NY)), d)

    def send_far(src, dst, sem, to):
        @pl.when(is_own)
        def _():
            pltpu.make_async_copy(src, dst, sem).start()

        @pl.when(jnp.logical_not(is_own))
        def _():
            pltpu.make_async_remote_copy(src, dst, ssem, sem, device_id=to, device_id_type=MESH).start()

        coming[id(sem), None] = src, sem

    send_far(xpad, x8.at[fi], s_xf, at(fy, fk, fx, fi))

    got(s_xy, *range(1, NY))
    send(xg.at[k], xg.at[k], s_xk, at(kk=1 - k))
    for d in range(1, NY):
        ty = other(y, d, NY)
        send(wst.at[ty], wg.at[y], s_w, at(yy=ty), d)
    for j in range(NY):
        unfold(xu, (k,), FP * j, xg[k, j])
    for d in (2, 1, 3, 0):
        th[d] = dot(rp[k, pl.ds(pl.multiple_of(XF * other(x, d, NX), 16), XF), :], xu[k])
    got(s_xk)
    for j in range(NY):
        unfold(xu, (1 - k,), FP * j, xg[1 - k, j])
    for d in (2, 1, 3, 0):
        tx_ = other(x, d, NX)
        t = th[d] + dot(rp[1 - k, pl.ds(pl.multiple_of(XF * tx_, 16), XF), :], xu[1 - k])
        ts[d, 0:XF, :] = t[:, 0:128]
        for i in range(8):
            ts[d, XF + 9 * i : XF + 9 * i + 9, 0:64] = t[F * i : F * i + 9, 128:192]
            ts[d, XF + 9 * i : XF + 9 * i + 9, 64:128] = t[F * i + 9 : F * i + F, 128:192]
        if d:
            send(ts.at[d], tr.at[d], s_t, at(xx=tx_), d)
    got(s_xf)
    for d in range(1, NZ):
        send(x8.at[z], x8.at[z], s_x8, at(zz=other(z, d, NZ)), d)
    got(s_w, *range(1, NY))
    part = dot(xu[k], wg[...].reshape(NY * FP, CY), TN)
    for q in range(8):
        dr[q] = part[DR * q : DR * (q + 1), :]
    for d in range(1, 8):
        tx_, tk_ = other(x, d // 2, NX), other(k, d % 2, NK)
        send(dr.at[2 * tx_ + tk_], drr.at[d], s_dx, at(xx=tx_, kk=tk_), d)
    got(s_x8, *range(1, 8))
    for i in range(8):
        unfold(x8c, (), F * i, x8[i])
    got(s_t, *range(1, NX))
    ts[0] = ts[0] + tr[1] + tr[2] + tr[3]
    tx[:, 0:128] = ts[0, 0:XF, :]
    for i in range(8):
        tx[F * i : F * i + 9, 128:192] = ts[0, XF + 9 * i : XF + 9 * i + 9, 0:64]
        tx[F * i + 9 : F * i + F, 128:192] = ts[0, XF + 9 * i : XF + 9 * i + 9, 64:128]
    inner = dot(x8c[...], tx[...], TN)
    for q in range(4):
        ar[q] = inner[SR * q : SR * (q + 1), 0:128]
    for q in range(2):
        ar[4 + q] = inner[128 + SR * q : 128 + SR * (q + 1), 0:128]
        ar[6 + q] = jnp.zeros((SR, 128), F32)
        ar[6 + q, :, 0:64] = inner[128 + SR * q : 128 + SR * (q + 1), 128:192]
    for d in range(1, 8):
        tx_, tk_ = other(x, d // 2, NX), other(k, d % 2, NK)
        send(ar.at[2 * tx_ + tk_], arr.at[d], s_ar, at(xx=tx_, kk=tk_), d)
    q_own = 2 * x + k
    got(s_dx, *range(1, 8))
    total = dr[q_own]
    for d in range(1, 8):
        total = total + drr[d]
    d1[...] = total
    for d in range(1, NZ):
        send(d1, dzr.at[d], s_dz, at(zz=other(z, d, NZ)), d)

    got(s_ar, *range(1, 8))
    total = ar[q_own]
    for d in range(1, 8):
        total = total + arr[d]
    a1[...] = total
    for d in range(1, NZ):
        send(a1, azr.at[d], s_az, at(zz=other(z, d, NZ)), d)
    for i in range(8):
        tp[i, 0:F, :] = ts[0, F * i : F * (i + 1), :]
        tp[i, F : F + 9, :] = ts[0, XF + 9 * i : XF + 9 * i + 9, :]
    for d in range(1, NZ):
        tz = other(z, d, NZ)
        send(tp.at[tz], tzr.at[d], s_tz, at(zz=tz), d)
    got(s_dz, *range(1, NZ))
    total = d1[...]
    for d in range(1, NZ):
        total = total + dzr[d]
    dyr[y] = total
    for d in range(1, NY):
        send(dyr.at[y], dyr.at[y], s_dy, at(yy=other(y, d, NY)), d)

    got(s_az, *range(1, NZ))
    total = a1[...]
    for d in range(1, NZ):
        total = total + azr[d]
    ayr[y] = total
    for d in range(1, NY):
        send(ayr.at[y], ayr.at[y], s_ay, at(yy=other(y, d, NY)), d)
    got(s_tz, *range(1, NZ))
    piece = tp[z]
    for d in range(1, NZ):
        piece = piece + tzr[d]
    pz[z] = piece
    for d in range(1, NZ):
        send(pz.at[z], pz.at[z], s_pz, at(zz=other(z, d, NZ)), d)
    send_far(pz.at[z], pc_out.at[gk, gy], s_pf, at(gy, gk, gx, gz))
    got(s_dy, *range(1, NY))
    pd_out[k, x] = dyr[...]
    for d in range(1, NX):
        send(pd_out.at[k, x], pd_out.at[k, x], s_d, at(xx=other(x, d, NX)), d)


    got(s_ay, *range(1, NY))
    total = ayr[0]
    for j in range(1, NY):
        total = total + ayr[j]
    asum[...] = total
    s_out[q_own] = total
    for d in range(1, 8):
        send(asum, s_out.at[q_own], s_s, at(xx=other(x, d // 2, NX), kk=other(k, d % 2, NK)), d)
    got(s_pz, *range(1, NZ))
    for i in range(8):
        prc[F * i : F * (i + 1), :] = pz[i, 0:F, :]
        prc[XF + 9 * i : XF + 9 * i + 9, :] = pz[i, F : F + 9, :]
    pr_out[x] = prc[...]
    for d in range(1, NX):
        send(prc, pr_out.at[x], s_px, at(xx=other(x, d, NX)), d)
    got(s_pf)
    for d in range(1, NY):
        send(pc_out.at[k, y], pc_out.at[k, y], s_pc, at(yy=other(y, d, NY)), d)
    got(s_d, *range(1, NX))
    send(pd_out.at[k], pd_out.at[k], s_dk, at(kk=1 - k))

    got(s_s, *range(1, 8))
    h = 64
    top = s_out[0:4].reshape(128, 128)
    low = s_out[4:6].reshape(h, 128)
    end = s_out[6:8].reshape(h, 128)[:, 0:h]
    eye = (
        lax.broadcasted_iota(jnp.int32, (B, B), 0) == lax.broadcasted_iota(jnp.int32, (B, B), 1)
    ).astype(F32)
    inv_out[0:128, 0:128] = 0.5 * (top + top.T)
    inv_out[128:192, 0:128] = low
    inv_out[0:128, 128:192] = low.T
    inv_out[128:192, 128:192] = 0.5 * (end + end.T)
    inv_out[...] = inv_out[...] + eye
    for n in range(3):
        pivot_block(inv_out, h, n)
        if n == 0:
            got(s_pc, *range(1, 8))
            send(pc_out.at[k], pc_out.at[k], s_pck, at(kk=1 - k))
    got(s_px, *range(1, NX))
    got(s_pck)
    got(s_dk)
    for cp in sent:
        cp.wait_send()

    @pl.when(jnp.logical_not(is_own))
    def _():
        pltpu.make_async_copy(xpad, xpad, ssem).wait()
        pltpu.make_async_copy(xpad, xpad, ssem).wait()


def update_kernel(inv, pr, pc, pd, cov, w, labels, cov_out, w_out, pcc, dd, prc, pco):
    y = lax.axis_index("y")
    k = lax.axis_index("k")
    for r in range(16):
        unfold(pcc, (), F * r, pc[r % 2, r // 2])
    for j in range(NX):
        prc[j, :, 0:128] = pr[j, 0:XF, :]
        for i in range(8):
            prc[j, F * i : F * i + 9, 128:192] = pr[j, XF + 9 * i : XF + 9 * i + 9, 0:64]
            prc[j, F * i + 9 : F * i + F, 128:192] = pr[j, XF + 9 * i : XF + 9 * i + 9, 64:128]
    pco[...] = jnp.zeros_like(pco)
    unfold(pco, (), 0, pc[k, y])
    named = jnp.broadcast_to(labels[...].astype(F32), (128, B)).T
    lane = lax.broadcasted_iota(jnp.int32, (B, 128), 1).astype(F32)
    for j in range(NY):
        for q in range(8):
            at = slice(DR * q, DR * (q + 1))
            dd[at, CY * j : CY * (j + 1)] = (named[at] == lane[at] + float(CY * j)).astype(F32) - pd[q % 2, q // 2, j]
    gain = dot(pcc[...], inv[...])
    cov_out[...] = cov[...] - dot(gain, prc[...].reshape(RF, B), NT)
    own = dot(pco[...], inv[...])
    w_out[...] = w[...] + dot(own, dd[...])[0:F]


def vmem(shape):
    return pltpu.VMEM(shape, F32)


def on_device(covariance, samples, labels, weights):
    in_vmem = pl.BlockSpec(memory_space=pltpu.VMEM)
    cov_t = covariance.T
    sems = lambda n: pltpu.SemaphoreType.DMA((n,))
    one = pltpu.SemaphoreType.DMA
    inv, pr, pc, pd, cov_in, w_in = pl.pallas_call(
        exchange_kernel,
        name="exchange",
        out_shape=tuple(
            jax.ShapeDtypeStruct(shape, F32)
            for shape in ((B, B), (NX, XR, 128), (2, NY, PP, 128), (2, NX, NY, DR, CY), (CF, RF), (F, C))
        ),
        in_specs=[pl.BlockSpec(memory_space=pltpu.HBM)] * 3,
        out_specs=(in_vmem,) * 6,
        scratch_shapes=[
            vmem((8, SR, 128)), vmem((F, B)), vmem((16 * FP, RF)), vmem((2, RF, NY * FP)),
            vmem((PP, 128)), vmem((NY, FP, CY)), vmem((2, NY, PP, 128)), vmem((2, NY * FP, B)),
            vmem((8, PP, 128)), vmem((XF, B)), vmem((NY, FP, CY)), vmem((NX, XF, B)),
            vmem((NX, XR, 128)), vmem((NX, XR, 128)), vmem((XF, B)), vmem((NZ, PP, 128)),
            vmem((NZ, PP, 128)), vmem((NZ, PP, 128)), vmem((XR, 128)),
            vmem((8, SR, 128)), vmem((8, SR, 128)), vmem((SR, 128)), vmem((NZ, SR, 128)), vmem((NY, SR, 128)),
            vmem((SR, 128)),
            vmem((8, DR, 128)), vmem((8, DR, 128)), vmem((DR, 128)), vmem((NZ, DR, 128)), vmem((NY, DR, 128)),
            sems(3), one, sems(8), one, one, sems(8), sems(8), sems(4), sems(8), sems(8), sems(8), sems(8), sems(8),
            one, sems(8), one, sems(4), sems(8), sems(4), one, sems(8), sems(8), sems(8),
        ],
        compiler_params=pltpu.CompilerParams(
            collective_id=0, has_side_effects=True, vmem_limit_bytes=40 * 2**20
        ),
    )(cov_t, samples.T, weights)
    cov_new, w_new = pl.pallas_call(
        update_kernel,
        name="update",
        out_shape=(jax.ShapeDtypeStruct((CF, RF), F32), jax.ShapeDtypeStruct((F, C), F32)),
        in_specs=[in_vmem] * 7,
        out_specs=(in_vmem,) * 2,
        scratch_shapes=[vmem((CF, B)), vmem((B, C)), vmem((NX, XF, B)), vmem((FP, B))],
        compiler_params=pltpu.CompilerParams(vmem_limit_bytes=40 * 2**20),
    )(inv, pr, pc, pd, cov_in, w_in, labels.reshape(1, B))
    return cov_new.T, w_new


def solution(mesh):
    finer = Mesh(mesh.devices.reshape(NY, NK, NX, NZ), ("y", "k", "x", "z"))
    row, col, both = ("y", "k"), ("x", "z"), ("x", "z", "y", "k")
    in_specs = (P(row, col), P(None, both), P(), P(both, None))
    out_specs = (P(row, col), P(both, None))
    return jax.shard_map(on_device, mesh=finer, in_specs=in_specs, out_specs=out_specs, check_vma=False)
```
